32 devices in a mesh: pair: 4 (over y, core), virt: 8 (over z, x).
Axes of the slice: x: 2, y: 2, z: 4, core: 2. Of those that a mesh axis runs over, the one named last changes fastest.
Arguments:
- amplitudes: float32 [4096, 1024], P('pair', 'virt'), may hold values from -6 to 6
- integrals: float32 [8192, 1024], P('virt', 'pair'), may hold values from -0.54 to 0.54
- residual_in: float32 [4096, 8192], P('pair', 'virt'), may hold values from -6 to 6
- pair_irrep: int32 [4096], P('pair'), may hold values from 0 to 7
- ab_irrep: int32 [8192], P('virt'), may hold values from 0 to 7
- cd_irrep: int32 [1024], replicated, may hold values from 0 to 7, as said below
Outputs:
- residual: float32 [4096, 8192], P('pair', 'virt')
The draws below stay inside these ranges and needn't reach their ends.
Inputs may be any that keep to these rules, and one draw needn't show every extreme that they name: `pair_irrep`: irrep labels. `ab_irrep`: irrep labels. `cd_irrep`: in every aligned block of 8 consecutive cd of the window, each of the 8 irreps labels exactly one cd.
All inputs are finite; a program needn't handle non-finite values.
Results may differ from the reference program's by a relative error of at most 0.00005.
Values sent between devices are 32-bit elements; how exact they have to be, the bound alone decides.
A program may use at most 64 MiB of HBM per device.

```python
import jax
import jax.numpy as jnp
from jax import lax

CD = 1024
PAIRS = 4096
AB = 8192


def draw_cd_irrep(key, part):
    blocks = CD // 8
    scores = jax.random.randint(key, (blocks, 8), 0, 1048576) * 8 + jnp.arange(8, dtype=jnp.int32)[None, :]
    order = jnp.argsort(scores, axis=1)
    return order.reshape(CD).astype(jnp.int32)


def plant(entries, rng, smallest, largest):
    shape = entries.shape
    spot = [jax.random.randint(jax.random.fold_in(rng, axis), (), 0, shape[axis]) for axis in range(len(shape))]
    entries = entries.at[tuple(spot)].set(smallest)
    longest = shape.index(max(shape))
    spot[longest] = (spot[longest] + 1) % shape[longest]
    return entries.at[tuple(spot)].set(largest)


def levels(own_key, shape, pieces, low, top_value):
    def one(position, parts):
        draws = jax.random.uniform(jax.random.fold_in(jax.random.fold_in(own_key, 6), position), (parts,), jnp.float32, low / len(pieces), top_value / len(pieces))
        return jnp.repeat(jnp.exp(draws), shape[position] // parts).reshape((-1,) + (1,) * (len(shape) - position - 1))

    level = one(*pieces[0])
    for cut in pieces[1:]:
        level = level * one(*cut)
    return level


def noise(own_key, extent, width, bound, pieces=(), kind=jnp.bfloat16):
    loudness = levels(own_key, extent, pieces, -0.22, 0.18) if pieces else 1.0
    array = jax.random.normal(own_key, extent, jnp.float32) * width * loudness
    return jnp.minimum(jnp.maximum(array, -bound), bound).astype(kind)


def setup_inputs(seed: int = 0) -> dict:
    streams_of = jax.random.split(jax.random.key(seed), 7)
    amplitudes = noise(streams_of[0], (PAIRS, CD), 1.0, 6.0, ((0, 4), (1, 8)), jnp.float32)
    integrals = noise(streams_of[1], (AB, CD), 0.09, 0.54, ((0, 8), (1, 4)), jnp.float32)
    residual_in = noise(streams_of[2], (PAIRS, AB), 1.0, 6.0, ((0, 4), (1, 8)), jnp.float32)
    pair_irrep = plant(jax.random.randint(streams_of[3], (PAIRS,), 0, 8), jax.random.fold_in(streams_of[3], 1), 0, 7).astype(jnp.int32)
    ab_irrep = plant(jax.random.randint(streams_of[4], (AB,), 0, 8), jax.random.fold_in(streams_of[4], 1), 0, 7).astype(jnp.int32)
    cd_irrep = draw_cd_irrep(jax.random.fold_in(streams_of[6], 71), 0)
    return {"amplitudes": amplitudes, "integrals": integrals, "residual_in": residual_in, "pair_irrep": pair_irrep, "ab_irrep": ab_irrep, "cd_irrep": cd_irrep}


def reference(amplitudes, integrals, residual_in, pair_irrep, ab_irrep, cd_irrep):
    masked_t = jnp.where(pair_irrep[:, None] == cd_irrep[None, :], amplitudes, jnp.float32(0.0))
    masked_v = jnp.where(ab_irrep[:, None] == cd_irrep[None, :], integrals, jnp.float32(0.0))
    ladder = lax.dot_general(masked_t, masked_v, (((1,), (1,)), ((), ())), precision=lax.Precision.HIGHEST, preferred_element_type=jnp.float32)
    return residual_in + ladder
```

```python
import functools

import jax
import jax.numpy as jnp
from jax import lax
from jax.experimental import pallas as pl
from jax.experimental.pallas import tpu as pltpu
from jax.sharding import PartitionSpec as P

IRREPS = 8
LANES = 128
MESH = pl.DeviceIdType.MESH


def pieces(x):
    high = x.astype(jnp.bfloat16)
    low = (x - high.astype(jnp.float32)).astype(jnp.bfloat16)
    return high, low


def nth_other(n, me, step):
    flip = me // (n // 2)
    mine = me + flip * (n - 1 - 2 * me)
    other = step + (step + n - mine) // n
    return other + flip * (n - 1 - 2 * other)


def irrep_row(rows_ref, first, count):
    n = count // LANES
    return jnp.concatenate([rows_ref[pl.ds(first + k, 1), :] for k in range(n)], axis=1)


def pick(cd_row, values, own_row):
    width = values.shape[1]
    blocks = width // IRREPS
    block = lax.broadcasted_iota(jnp.int32, (blocks, width), 0)
    lane_block = lax.shift_right_logical(lax.broadcasted_iota(jnp.int32, (blocks, width), 1), 3)
    slabs = [
        jnp.where((block == lane_block) & (cd_row == g), jnp.float32(1), jnp.float32(0))
        for g in range(IRREPS)
    ]
    sorter = jnp.concatenate(slabs, axis=0).astype(jnp.bfloat16)
    high, low = pieces(values)
    across = (((1,), (1,)), ((), ()))
    by_irrep = lax.dot_general(
        sorter, high, across, preferred_element_type=jnp.float32
    ) + lax.dot_general(sorter, low, across, preferred_element_type=jnp.float32)
    chosen = by_irrep[:blocks]
    for g in range(1, IRREPS):
        chosen = jnp.where(own_row == g, by_irrep[g * blocks : (g + 1) * blocks], chosen)
    return chosen


def gather_kernel(
    n_pair, n_virt, parts,
    t_hbm, v_hbm, pi_ref, ai_ref, cdt_ref, cdv_ref,
    t_out, v_out,
    t_own, v_own, t_all, v_all,
    load_sem, t_send, t_recv, tf_send, v_send, v_recv, vf_send,
):
    p, v = lax.axis_index("pair"), lax.axis_index("virt")
    a, b = v // 2, v % 2
    c, k = p // 2, p % 2
    n_a, n_c = n_virt // 2, n_pair // 2
    rows, t_width = t_own.shape
    ab, v_width = v_own.shape
    t_blocks, v_blocks = t_width // IRREPS, v_width // IRREPS

    load_t = pltpu.make_async_copy(t_hbm, t_own, load_sem.at[0])
    load_v = pltpu.make_async_copy(v_hbm, v_own, load_sem.at[1])
    load_t.start()
    load_v.start()

    barrier = pltpu.get_barrier_semaphore()

    def greet(dev):
        pl.semaphore_signal(barrier, inc=1, device_id=dev, device_id_type=MESH)

    far_a = [nth_other(n_a, a, s) for s in range(n_a - 1)]
    far_c = [nth_other(n_c, c, s) for s in range(n_c - 1)]
    for o in far_a:
        greet((p, o * 2 + b))
    greet((p, a * 2 + 1 - b))
    for o in far_c:
        greet((o * 2 + k, v))
    greet((c * 2 + 1 - k, v))

    def copy(ref, owner, blocks, part, span, send, recv, dev):
        at = ref.at[pl.ds(pl.multiple_of(owner * blocks, blocks), blocks), pl.ds(part * span, span)]
        return pltpu.make_async_remote_copy(
            src_ref=at, dst_ref=at, send_sem=send, recv_sem=recv, device_id=dev, device_id_type=MESH
        )

    t_span, v_span = rows // parts, ab // parts

    def t_copy(owner, part, send, dev):
        return copy(t_all, owner, t_blocks, part, t_span, send, t_recv.at[owner * parts + part], dev)

    def v_copy(owner, part, send, dev):
        return copy(v_all, owner, v_blocks, part, v_span, send, v_recv.at[owner * parts + part], dev)

    cdt_row = irrep_row(cdt_ref, v * t_width // LANES, t_width) if t_width % LANES == 0 else cdt_ref[pl.ds(v, 1), :]
    cdv_row = irrep_row(cdv_ref, p * v_width // LANES, v_width) if v_width % LANES == 0 else cdv_ref[pl.ds(p, 1), :]

    load_t.wait()
    sent = []
    for h in range(parts):
        own = irrep_row(pi_ref, h * t_span // LANES, t_span)
        t_all[pl.ds(pl.multiple_of(v * t_blocks, t_blocks), t_blocks), h * t_span : (h + 1) * t_span] = pick(
            cdt_row, t_own[h * t_span : (h + 1) * t_span, :], own
        )
        if h == 0:
            pl.semaphore_wait(barrier, n_a + n_c)
        for s in reversed(range(n_a - 1)):
            sent.append(t_copy(v, h, t_send.at[s, h], (p, far_a[s] * 2 + b)))
            sent[-1].start()
        sent.append(t_copy(v, h, t_send.at[n_a - 1, h], (p, a * 2 + 1 - b)))
        sent[-1].start()

    load_v.wait()
    for h in range(parts):
        own = irrep_row(ai_ref, h * v_span // LANES, v_span)
        v_all[pl.ds(pl.multiple_of(p * v_blocks, v_blocks), v_blocks), h * v_span : (h + 1) * v_span] = pick(
            cdv_row, v_own[h * v_span : (h + 1) * v_span, :], own
        )
        for s in reversed(range(n_c - 1)):
            sent.append(v_copy(p, h, v_send.at[s, h], (far_c[s] * 2 + k, v)))
            sent[-1].start()
        sent.append(v_copy(p, h, v_send.at[n_c - 1, h], (c * 2 + 1 - k, v)))
        sent[-1].start()

    for h in range(parts):
        for s in range(n_a - 1):
            dev = (p, a * 2 + 1 - b)
            onward = t_copy(far_a[s] * 2 + b, h, tf_send.at[s, h], dev)
            onward.wait_recv()
            onward.start()
            sent.append(onward)
        for s in range(n_c - 1):
            dev = (c * 2 + 1 - k, v)
            onward = v_copy(far_c[s] * 2 + k, h, vf_send.at[s, h], dev)
            onward.wait_recv()
            onward.start()
            sent.append(onward)

    for h in range(parts):
        span = slice(h * v_span, (h + 1) * v_span)
        for o in range(n_c):
            v_copy(o * 2 + 1 - k, h, v_send.at[0, h], (p, v)).wait_recv()
        high, low = pieces(v_all[:, span])
        v_out[: high.shape[0], span] = high
        v_out[high.shape[0] :, span] = low
    for h in range(parts):
        span = slice(h * t_span, (h + 1) * t_span)
        for o in range(n_a):
            t_copy(o * 2 + 1 - b, h, t_send.at[0, h], (p, v)).wait_recv()
        t_out[:, span] = t_all[:, span]
    for s in sent:
        s.wait_send()


def gather(n_pair, n_virt, t, v, pi, ai, cd, cdt, cdv):
    parts = 2
    rows, t_width = t.shape
    ab, v_width = v.shape
    blocks = cd // IRREPS
    vmem, dma = pltpu.VMEM, pltpu.SemaphoreType.DMA
    n_a, n_c = n_virt // 2, n_pair // 2
    return pl.pallas_call(
        functools.partial(gather_kernel, n_pair, n_virt, parts),
        out_shape=(
            jax.ShapeDtypeStruct((blocks, rows), jnp.float32),
            jax.ShapeDtypeStruct((2 * blocks, ab), jnp.bfloat16),
        ),
        in_specs=[pl.BlockSpec(memory_space=pltpu.HBM)] * 2 + [pl.BlockSpec(memory_space=vmem)] * 4,
        out_specs=(pl.BlockSpec(memory_space=vmem),) * 2,
        scratch_shapes=[
            vmem((rows, t_width), jnp.float32),
            vmem((ab, v_width), jnp.float32),
            vmem((blocks, rows), jnp.float32),
            vmem((blocks, ab), jnp.float32),
            dma((2,)),
            dma((n_a, parts)),
            dma((n_virt * parts,)),
            dma((max(n_a - 1, 1), parts)),
            dma((n_c, parts)),
            dma((n_pair * parts,)),
            dma((max(n_c - 1, 1), parts)),
        ],
        compiler_params=pltpu.CompilerParams(
            collective_id=0, has_side_effects=True, vmem_limit_bytes=16 * 1024 * 1024
        ),
        name="pick_and_gather",
    )(t, v, pi, ai, cdt, cdv)


def ladder_kernel(t_ref, v_ref, pi_ref, ai_ref, r_ref, out_ref):
    blocks, tile = t_ref.shape
    ab = r_ref.shape[1]
    step = pl.program_id(0)
    th, tl = pieces(t_ref[...].T)
    left = jnp.concatenate([th, tl, th, tl], axis=1)
    vh, vl = v_ref[:blocks, :], v_ref[blocks:, :]
    right = jnp.concatenate([vh, vh, vl, vl], axis=0)
    total = lax.dot_general(left, right, (((1,), (0,)), ((), ())), preferred_element_type=jnp.float32)
    ab_row = irrep_row(ai_ref, 0, ab)
    for m in range(tile // LANES):
        row = pi_ref[pl.ds(step * (tile // LANES) + m, 1), :]
        column = jnp.broadcast_to(row, (LANES, LANES)).T
        same = jnp.concatenate([column] * (ab // LANES), axis=1) == ab_row
        at = slice(m * LANES, (m + 1) * LANES)
        out_ref[at, :] = r_ref[at, :] + jnp.where(same, total[at, :], jnp.float32(0))


def ladder(t_all, v_all, pi, ai, residual):
    rows, ab = residual.shape
    blocks = t_all.shape[0]
    tile = 256
    whole = lambda i: (0, 0)
    return pl.pallas_call(
        ladder_kernel,
        out_shape=jax.ShapeDtypeStruct((rows, ab), jnp.float32),
        grid=(rows // tile,),
        in_specs=[
            pl.BlockSpec((blocks, tile), lambda i: (0, i)),
            pl.BlockSpec(v_all.shape, whole),
            pl.BlockSpec(pi.shape, whole),
            pl.BlockSpec(ai.shape, whole),
            pl.BlockSpec((tile, ab), lambda i: (i, 0)),
        ],
        out_specs=pl.BlockSpec((tile, ab), lambda i: (i, 0)),
        compiler_params=pltpu.CompilerParams(vmem_limit_bytes=24 * 1024 * 1024),
        name="ladder",
    )(t_all, v_all, pi, ai, residual)


def solution(mesh):
    n_pair, n_virt = mesh.shape["pair"], mesh.shape["virt"]

    def shards(amplitudes, integrals, residual_in, pair_irrep, ab_irrep, cd_irrep):
        cd = cd_irrep.shape[0]
        pi, ai = pair_irrep.reshape(-1, LANES), ab_irrep.reshape(-1, LANES)

        def cd_rows(width):
            return cd_irrep.reshape(-1, LANES if width % LANES == 0 else width)

        t_all, v_all = gather(
            n_pair, n_virt, amplitudes, integrals, pi, ai, cd,
            cd_rows(amplitudes.shape[1]), cd_rows(integrals.shape[1]),
        )
        return ladder(t_all, v_all, pi, ai, residual_in)

    placed = (P("pair", "virt"), P("virt", "pair"), P("pair", "virt"), P("pair"), P("virt"), P())
    return jax.shard_map(
        shards, mesh=mesh, in_specs=placed, out_specs=P("pair", "virt"), check_vma=False
    )
```

```python
import functools

import jax
import jax.numpy as jnp
from jax import lax
from jax.experimental import pallas as pl
from jax.experimental.pallas import tpu as pltpu
from jax.sharding import PartitionSpec as P

IRREPS = 8
LANES = 128
MESH = pl.DeviceIdType.MESH


def pieces(x):
    high = x.astype(jnp.bfloat16)
    low = (x - high.astype(jnp.float32)).astype(jnp.bfloat16)
    return high, low


def nth_other(n, me, step):
    flip = me // (n // 2)
    mine = me + flip * (n - 1 - 2 * me)
    other = step + (step + n - mine) // n
    return other + flip * (n - 1 - 2 * other)


def irrep_row(rows_ref, first, count):
    n = count // LANES
    return jnp.concatenate([rows_ref[pl.ds(first + k, 1), :] for k in range(n)], axis=1)


def pick(cd_row, values, own_row):
    width = values.shape[1]
    blocks = width // IRREPS
    block = lax.broadcasted_iota(jnp.int32, (blocks, width), 0)
    lane_block = lax.shift_right_logical(lax.broadcasted_iota(jnp.int32, (blocks, width), 1), 3)
    slabs = [
        jnp.where((block == lane_block) & (cd_row == g), jnp.float32(1), jnp.float32(0))
        for g in range(IRREPS)
    ]
    sorter = jnp.concatenate(slabs, axis=0).astype(jnp.bfloat16)
    high, low = pieces(values)
    across = (((1,), (1,)), ((), ()))
    if width == LANES:
        both = jnp.concatenate([high, low], axis=1)
        twice = jnp.concatenate([sorter, sorter], axis=1)
        by_irrep = lax.dot_general(twice, both, across, preferred_element_type=jnp.float32)
    else:
        by_irrep = lax.dot_general(
            sorter, high, across, preferred_element_type=jnp.float32
        ) + lax.dot_general(sorter, low, across, preferred_element_type=jnp.float32)
    chosen = by_irrep[:blocks]
    for g in range(1, IRREPS):
        chosen = jnp.where(own_row == g, by_irrep[g * blocks : (g + 1) * blocks], chosen)
    return chosen


def ladder_kernel(
    n_pair, n_virt, parts,
    t_hbm, v_hbm, r_hbm, pi_hbm, ai_hbm, cdt_hbm, cdv_hbm,
    out_ref,
    t_own, v_own, pi_ref, ai_ref, cdt_ref, cdv_ref, t_all, v_all, right_ref, column_ref,
    load_sem, t_send, t_recv, tf_send, v_send, v_recv, vf_send,
):
    p, v = lax.axis_index("pair"), lax.axis_index("virt")
    a, b = v // 2, v % 2
    c, k = p // 2, p % 2
    n_a, n_c = n_virt // 2, n_pair // 2
    rows, t_width = t_own.shape
    ab, v_width = v_own.shape
    t_blocks, v_blocks = t_width // IRREPS, v_width // IRREPS
    blocks = t_all.shape[0]

    barrier = pltpu.get_barrier_semaphore()

    def greet(dev):
        pl.semaphore_signal(barrier, inc=1, device_id=dev, device_id_type=MESH)

    far_a = [nth_other(n_a, a, s) for s in range(n_a - 1)]
    far_c = [nth_other(n_c, c, s) for s in range(n_c - 1)]
    for o in far_a:
        greet((p, o * 2 + b))
    greet((p, a * 2 + 1 - b))
    for o in far_c:
        greet((o * 2 + k, v))
    greet((c * 2 + 1 - k, v))

    loads = [
        pltpu.make_async_copy(src, dst, load_sem.at[n])
        for n, (src, dst) in enumerate(
            [
                (t_hbm, t_own), (cdt_hbm, cdt_ref), (pi_hbm, pi_ref),
                (v_hbm, v_own), (cdv_hbm, cdv_ref), (ai_hbm, ai_ref), (r_hbm, out_ref),
            ]
        )
    ]
    for load in loads:
        load.start()

    def copy(ref, owner, count, part, span, send, recv, dev):
        at = ref.at[pl.ds(pl.multiple_of(owner * count, count), count), pl.ds(part * span, span)]
        return pltpu.make_async_remote_copy(
            src_ref=at, dst_ref=at, send_sem=send, recv_sem=recv, device_id=dev, device_id_type=MESH
        )

    t_span, v_span = rows // parts, ab // parts

    def t_copy(owner, part, send, dev):
        return copy(t_all, owner, t_blocks, part, t_span, send, t_recv.at[owner * parts + part], dev)

    def v_copy(owner, part, send, dev):
        return copy(v_all, owner, v_blocks, part, v_span, send, v_recv.at[owner * parts + part], dev)

    for load in loads[:3]:
        load.wait()
    cdt_row = irrep_row(cdt_ref, v * t_width // LANES, t_width) if t_width % LANES == 0 else cdt_ref[pl.ds(v, 1), :]
    sent = []
    for h in range(parts):
        own = irrep_row(pi_ref, h * t_span // LANES, t_span)
        t_all[pl.ds(pl.multiple_of(v * t_blocks, t_blocks), t_blocks), h * t_span : (h + 1) * t_span] = pick(
            cdt_row, t_own[h * t_span : (h + 1) * t_span, :], own
        )
        if h == 0:
            pl.semaphore_wait(barrier, n_a + n_c)
        for s in reversed(range(n_a - 1)):
            sent.append(t_copy(v, h, t_send.at[s, h], (p, far_a[s] * 2 + b)))
            sent[-1].start()
        sent.append(t_copy(v, h, t_send.at[n_a - 1, h], (p, a * 2 + 1 - b)))
        sent[-1].start()

    for load in loads[3:6]:
        load.wait()
    cdv_row = irrep_row(cdv_ref, p * v_width // LANES, v_width) if v_width % LANES == 0 else cdv_ref[pl.ds(p, 1), :]
    for h in range(parts):
        own = irrep_row(ai_ref, h * v_span // LANES, v_span)
        v_all[pl.ds(pl.multiple_of(p * v_blocks, v_blocks), v_blocks), h * v_span : (h + 1) * v_span] = pick(
            cdv_row, v_own[h * v_span : (h + 1) * v_span, :], own
        )
        for s in reversed(range(n_c - 1)):
            sent.append(v_copy(p, h, v_send.at[s, h], (far_c[s] * 2 + k, v)))
            sent[-1].start()
        sent.append(v_copy(p, h, v_send.at[n_c - 1, h], (c * 2 + 1 - k, v)))
        sent[-1].start()

    for m in range(rows // LANES):
        labels = jnp.broadcast_to(pi_ref[m : m + 1, :], (LANES, LANES))
        column_ref[m * LANES : (m + 1) * LANES, :] = labels.T

    for h in range(parts):
        for s in range(n_a - 1):
            onward = t_copy(far_a[s] * 2 + b, h, tf_send.at[s, h], (p, a * 2 + 1 - b))
            onward.wait_recv()
            onward.start()
            sent.append(onward)
        for s in range(n_c - 1):
            onward = v_copy(far_c[s] * 2 + k, h, vf_send.at[s, h], (c * 2 + 1 - k, v))
            onward.wait_recv()
            onward.start()
            sent.append(onward)

    for h in range(parts):
        span = slice(h * v_span, (h + 1) * v_span)
        for o in range(n_c):
            v_copy(o * 2 + 1 - k, h, v_send.at[0, h], (p, v)).wait_recv()
        high, low = pieces(v_all[:, span])
        right_ref[:blocks, span] = high
        right_ref[blocks : 2 * blocks, span] = high
        right_ref[2 * blocks : 3 * blocks, span] = low
        right_ref[3 * blocks :, span] = low

    ab_row = irrep_row(ai_ref, 0, ab)
    loads[6].wait()
    for h in range(parts):
        for o in range(n_a):
            t_copy(o * 2 + 1 - b, h, t_send.at[0, h], (p, v)).wait_recv()
        for m in range(h * t_span // LANES, (h + 1) * t_span // LANES):
            at = slice(m * LANES, (m + 1) * LANES)
            high, low = pieces(t_all[:, at].T)
            left = jnp.concatenate([high, low, high, low], axis=1)
            total = jnp.dot(left, right_ref[...], preferred_element_type=jnp.float32)
            same = jnp.concatenate([column_ref[at, :]] * (ab // LANES), axis=1) == ab_row
            out_ref[at, :] += jnp.where(same, total, jnp.float32(0))
    for s in sent:
        s.wait_send()


def ladder(n_pair, n_virt, t, v, residual, pi, ai, cd, cdt, cdv):
    parts = 2
    rows, t_width = t.shape
    ab, v_width = v.shape
    blocks = cd // IRREPS
    vmem, dma = pltpu.VMEM, pltpu.SemaphoreType.DMA
    n_a, n_c = n_virt // 2, n_pair // 2
    operands = (t, v, residual, pi, ai, cdt, cdv)
    return pl.pallas_call(
        functools.partial(ladder_kernel, n_pair, n_virt, parts),
        out_shape=pltpu.VMEM((rows, ab), jnp.float32),
        in_specs=[pl.BlockSpec(memory_space=pltpu.HBM)] * len(operands),
        out_specs=pl.BlockSpec(memory_space=vmem),
        scratch_shapes=[
            vmem((rows, t_width), jnp.float32),
            vmem((ab, v_width), jnp.float32),
            vmem(pi.shape, jnp.int32),
            vmem(ai.shape, jnp.int32),
            vmem(cdt.shape, jnp.int32),
            vmem(cdv.shape, jnp.int32),
            vmem((blocks, rows), jnp.float32),
            vmem((blocks, ab), jnp.float32),
            vmem((4 * blocks, ab), jnp.bfloat16),
            vmem((rows, LANES), jnp.int32),
            dma((7,)),
            dma((n_a, parts)),
            dma((n_virt * parts,)),
            dma((max(n_a - 1, 1), parts)),
            dma((n_c, parts)),
            dma((n_pair * parts,)),
            dma((max(n_c - 1, 1), parts)),
        ],
        compiler_params=pltpu.CompilerParams(
            collective_id=0, has_side_effects=True, vmem_limit_bytes=24 * 1024 * 1024
        ),
        name="pick_gather_ladder",
    )(*[pltpu.with_memory_space_constraint(x, pltpu.HBM) for x in operands])


def write_kernel(parts, src, dst, sem):
    span = src.shape[0] // parts
    copies = [
        pltpu.make_async_copy(src.at[pl.ds(n * span, span), :], dst.at[pl.ds(n * span, span), :], sem.at[n])
        for n in range(parts)
    ]
    for c in copies:
        c.start()
    for c in copies:
        c.wait()


def write(x):
    parts = 8
    return pl.pallas_call(
        functools.partial(write_kernel, parts),
        out_shape=jax.ShapeDtypeStruct(x.shape, x.dtype),
        in_specs=[pl.BlockSpec(memory_space=pl.ANY)],
        out_specs=pl.BlockSpec(memory_space=pl.ANY),
        scratch_shapes=[pltpu.SemaphoreType.DMA((parts,))],
        name="write",
    )(x)


def solution(mesh):
    n_pair, n_virt = mesh.shape["pair"], mesh.shape["virt"]

    def shards(amplitudes, integrals, residual_in, pair_irrep, ab_irrep, cd_irrep):
        cd = cd_irrep.shape[0]
        pi, ai = pair_irrep.reshape(-1, LANES), ab_irrep.reshape(-1, LANES)

        def cd_rows(width):
            return cd_irrep.reshape(-1, LANES if width % LANES == 0 else width)

        return write(
            ladder(
                n_pair, n_virt, amplitudes, integrals, residual_in, pi, ai, cd,
                cd_rows(amplitudes.shape[1]), cd_rows(integrals.shape[1]),
            )
        )

    placed = (P("pair", "virt"), P("virt", "pair"), P("pair", "virt"), P("pair"), P("virt"), P())
    return jax.shard_map(
        shards, mesh=mesh, in_specs=placed, out_specs=P("pair", "virt"), check_vma=False
    )
```

```python
import functools

import jax
import jax.numpy as jnp
from jax import lax
from jax.experimental import pallas as pl
from jax.experimental.pallas import tpu as pltpu
from jax.sharding import PartitionSpec as P

IRREPS = 8
LANES = 128
MESH = pl.DeviceIdType.MESH


def pieces(x):
    high = x.astype(jnp.bfloat16)
    low = (x - high.astype(jnp.float32)).astype(jnp.bfloat16)
    return high, low


def nth_other(n, me, step):
    flip = me // (n // 2)
    mine = me + flip * (n - 1 - 2 * me)
    other = step + (step + n - mine) // n
    return other + flip * (n - 1 - 2 * other)


def irrep_row(rows_ref, first, count):
    n = count // LANES
    return jnp.concatenate([rows_ref[pl.ds(first + k, 1), :] for k in range(n)], axis=1)


def pick(cd_row, values, own_row):
    width = values.shape[1]
    blocks = width // IRREPS
    block = lax.broadcasted_iota(jnp.int32, (blocks, width), 0)
    lane_block = lax.shift_right_logical(lax.broadcasted_iota(jnp.int32, (blocks, width), 1), 3)
    slabs = [
        jnp.where((block == lane_block) & (cd_row == g), jnp.float32(1), jnp.float32(0))
        for g in range(IRREPS)
    ]
    sorter = jnp.concatenate(slabs, axis=0).astype(jnp.bfloat16)
    high, low = pieces(values)
    across = (((1,), (1,)), ((), ()))
    if width == LANES:
        both = jnp.concatenate([high, low], axis=1)
        twice = jnp.concatenate([sorter, sorter], axis=1)
        by_irrep = lax.dot_general(twice, both, across, preferred_element_type=jnp.float32)
    else:
        by_irrep = lax.dot_general(
            sorter, high, across, preferred_element_type=jnp.float32
        ) + lax.dot_general(sorter, low, across, preferred_element_type=jnp.float32)
    chosen = by_irrep[:blocks]
    for g in range(1, IRREPS):
        chosen = jnp.where(own_row == g, by_irrep[g * blocks : (g + 1) * blocks], chosen)
    return chosen


def ladder_kernel(
    n_pair, n_virt, parts,
    t_hbm, v_hbm, r_hbm, pi_hbm, ai_hbm, cdt_hbm, cdv_hbm,
    out_ref,
    t_own, v_own, pi_ref, ai_ref, cdt_ref, cdv_ref, t_all, v_all, right_ref, column_ref,
    load_sem, t_send, t_recv, tf_send, v_send, v_recv, vf_send,
):
    p, v = lax.axis_index("pair"), lax.axis_index("virt")
    a, b = v // 2, v % 2
    c, k = p // 2, p % 2
    n_a, n_c = n_virt // 2, n_pair // 2
    rows, t_width = t_own.shape
    ab, v_width = v_own.shape
    t_blocks, v_blocks = t_width // IRREPS, v_width // IRREPS
    blocks = t_all.shape[0]

    barrier = pltpu.get_barrier_semaphore()

    def greet(dev):
        pl.semaphore_signal(barrier, inc=1, device_id=dev, device_id_type=MESH)

    far_a = [nth_other(n_a, a, s) for s in range(n_a - 1)]
    far_c = [nth_other(n_c, c, s) for s in range(n_c - 1)]
    for o in far_a:
        greet((p, o * 2 + b))
    greet((p, a * 2 + 1 - b))
    for o in far_c:
        greet((o * 2 + k, v))
    greet((c * 2 + 1 - k, v))

    loads = [
        pltpu.make_async_copy(src, dst, load_sem.at[n])
        for n, (src, dst) in enumerate(
            [
                (t_hbm, t_own), (cdt_hbm, cdt_ref), (pi_hbm, pi_ref),
                (v_hbm, v_own), (cdv_hbm, cdv_ref), (ai_hbm, ai_ref), (r_hbm, out_ref),
            ]
        )
    ]
    for load in loads:
        load.start()

    def copy(ref, owner, count, part, span, send, recv, dev):
        at = ref.at[pl.ds(pl.multiple_of(owner * count, count), count), pl.ds(part * span, span)]
        return pltpu.make_async_remote_copy(
            src_ref=at, dst_ref=at, send_sem=send, recv_sem=recv, device_id=dev, device_id_type=MESH
        )

    t_span, v_span = rows // parts, ab // parts

    def t_copy(owner, part, send, dev):
        return copy(t_all, owner, t_blocks, part, t_span, send, t_recv.at[owner * parts + part], dev)

    def v_copy(owner, part, send, dev):
        return copy(v_all, owner, v_blocks, part, v_span, send, v_recv.at[owner * parts + part], dev)

    for load in loads[:3]:
        load.wait()
    cdt_row = irrep_row(cdt_ref, v * t_width // LANES, t_width) if t_width % LANES == 0 else cdt_ref[pl.ds(v, 1), :]
    sent = []
    for h in range(parts):
        own = irrep_row(pi_ref, h * t_span // LANES, t_span)
        t_all[pl.ds(pl.multiple_of(v * t_blocks, t_blocks), t_blocks), h * t_span : (h + 1) * t_span] = pick(
            cdt_row, t_own[h * t_span : (h + 1) * t_span, :], own
        )
        if h == 0:
            pl.semaphore_wait(barrier, n_a + n_c)
        for s in reversed(range(n_a - 1)):
            sent.append(t_copy(v, h, t_send.at[s, h], (p, far_a[s] * 2 + b)))
            sent[-1].start()
        sent.append(t_copy(v, h, t_send.at[n_a - 1, h], (p, a * 2 + 1 - b)))
        sent[-1].start()

    for load in loads[3:6]:
        load.wait()
    cdv_row = irrep_row(cdv_ref, p * v_width // LANES, v_width) if v_width % LANES == 0 else cdv_ref[pl.ds(p, 1), :]
    for h in range(parts):
        own = irrep_row(ai_ref, h * v_span // LANES, v_span)
        v_all[pl.ds(pl.multiple_of(p * v_blocks, v_blocks), v_blocks), h * v_span : (h + 1) * v_span] = pick(
            cdv_row, v_own[h * v_span : (h + 1) * v_span, :], own
        )
        for s in reversed(range(n_c - 1)):
            sent.append(v_copy(p, h, v_send.at[s, h], (far_c[s] * 2 + k, v)))
            sent[-1].start()
        sent.append(v_copy(p, h, v_send.at[n_c - 1, h], (c * 2 + 1 - k, v)))
        sent[-1].start()

    for m in range(rows // LANES):
        labels = jnp.broadcast_to(pi_ref[m : m + 1, :], (LANES, LANES))
        column_ref[m * LANES : (m + 1) * LANES, :] = labels.T

    for h in range(parts):
        for s in range(n_a - 1):
            onward = t_copy(far_a[s] * 2 + b, h, tf_send.at[s, h], (p, a * 2 + 1 - b))
            onward.wait_recv()
            onward.start()
            sent.append(onward)
        for s in range(n_c - 1):
            onward = v_copy(far_c[s] * 2 + k, h, vf_send.at[s, h], (c * 2 + 1 - k, v))
            onward.wait_recv()
            onward.start()
            sent.append(onward)

    for h in range(parts):
        span = slice(h * v_span, (h + 1) * v_span)
        for o in range(n_c):
            v_copy(o * 2 + 1 - k, h, v_send.at[0, h], (p, v)).wait_recv()
        high, low = pieces(v_all[:, span])
        right_ref[:blocks, span] = high
        right_ref[blocks : 2 * blocks, span] = high
        right_ref[2 * blocks : 3 * blocks, span] = low
        right_ref[3 * blocks :, span] = low

    ab_row = irrep_row(ai_ref, 0, ab)
    loads[6].wait()
    for h in range(parts):
        for o in range(n_a):
            t_copy(o * 2 + 1 - b, h, t_send.at[0, h], (p, v)).wait_recv()
        for m in range(h * t_span // LANES, (h + 1) * t_span // LANES):
            at = slice(m * LANES, (m + 1) * LANES)
            high, low = pieces(t_all[:, at].T)
            left = jnp.concatenate([high, low, high, low], axis=1)
            total = jnp.dot(left, right_ref[...], preferred_element_type=jnp.float32)
            same = jnp.concatenate([column_ref[at, :]] * (ab // LANES), axis=1) == ab_row
            out_ref[at, :] += jnp.where(same, total, jnp.float32(0))
    for s in sent:
        s.wait_send()


def ladder(n_pair, n_virt, t, v, residual, pi, ai, cd, cdt, cdv):
    parts = 2
    rows, t_width = t.shape
    ab, v_width = v.shape
    blocks = cd // IRREPS
    vmem, dma = pltpu.VMEM, pltpu.SemaphoreType.DMA
    n_a, n_c = n_virt // 2, n_pair // 2
    operands = (t, v, residual, pi, ai, cdt, cdv)
    return pl.pallas_call(
        functools.partial(ladder_kernel, n_pair, n_virt, parts),
        out_shape=pltpu.VMEM((rows, ab), jnp.float32),
        in_specs=[pl.BlockSpec(memory_space=pltpu.HBM)] * len(operands),
        out_specs=pl.BlockSpec(memory_space=vmem),
        scratch_shapes=[
            vmem((rows, t_width), jnp.float32),
            vmem((ab, v_width), jnp.float32),
            vmem(pi.shape, jnp.int32),
            vmem(ai.shape, jnp.int32),
            vmem(cdt.shape, jnp.int32),
            vmem(cdv.shape, jnp.int32),
            vmem((blocks, rows), jnp.float32),
            vmem((blocks, ab), jnp.float32),
            vmem((4 * blocks, ab), jnp.bfloat16),
            vmem((rows, LANES), jnp.int32),
            dma((7,)),
            dma((n_a, parts)),
            dma((n_virt * parts,)),
            dma((max(n_a - 1, 1), parts)),
            dma((n_c, parts)),
            dma((n_pair * parts,)),
            dma((max(n_c - 1, 1), parts)),
        ],
        compiler_params=pltpu.CompilerParams(
            collective_id=0, has_side_effects=True, vmem_limit_bytes=24 * 1024 * 1024
        ),
        name="pick_gather_ladder",
    )(*[pltpu.with_memory_space_constraint(x, pltpu.HBM) for x in operands])


def write_kernel(parts, src, dst, sem):
    span = src.shape[0] // parts
    copies = [
        pltpu.make_async_copy(src.at[pl.ds(n * span, span), :], dst.at[pl.ds(n * span, span), :], sem.at[n])
        for n in range(parts)
    ]
    for c in copies:
        c.start()
    for c in copies:
        c.wait()


def write(x):
    parts = 8
    return pl.pallas_call(
        functools.partial(write_kernel, parts),
        out_shape=jax.ShapeDtypeStruct(x.shape, x.dtype),
        in_specs=[pl.BlockSpec(memory_space=pl.ANY)],
        out_specs=pl.BlockSpec(memory_space=pl.ANY),
        scratch_shapes=[pltpu.SemaphoreType.DMA((parts,))],
        compiler_params=pltpu.CompilerParams(vmem_limit_bytes=1024 * 1024),
        name="write",
    )(pltpu.with_memory_space_constraint(x, pltpu.VMEM))


def solution(mesh):
    n_pair, n_virt = mesh.shape["pair"], mesh.shape["virt"]

    def shards(amplitudes, integrals, residual_in, pair_irrep, ab_irrep, cd_irrep):
        cd = cd_irrep.shape[0]
        pi, ai = pair_irrep.reshape(-1, LANES), ab_irrep.reshape(-1, LANES)

        def cd_rows(width):
            return cd_irrep.reshape(-1, LANES if width % LANES == 0 else width)

        return write(
            ladder(
                n_pair, n_virt, amplitudes, integrals, residual_in, pi, ai, cd,
                cd_rows(amplitudes.shape[1]), cd_rows(integrals.shape[1]),
            )
        )

    placed = (P("pair", "virt"), P("virt", "pair"), P("pair", "virt"), P("pair"), P("virt"), P())
    return jax.shard_map(
        shards, mesh=mesh, in_specs=placed, out_specs=P("pair", "virt"), check_vma=False
    )
```

```python
import functools

import jax
import jax.numpy as jnp
from jax import lax
from jax.experimental import pallas as pl
from jax.experimental.pallas import tpu as pltpu
from jax.sharding import PartitionSpec as P

IRREPS = 8
LANES = 128
MESH = pl.DeviceIdType.MESH


def pieces(x):
    high = x.astype(jnp.bfloat16)
    low = (x - high.astype(jnp.float32)).astype(jnp.bfloat16)
    return high, low


def nth_other(n, me, step):
    flip = me // (n // 2)
    mine = me + flip * (n - 1 - 2 * me)
    other = step + (step + n - mine) // n
    return other + flip * (n - 1 - 2 * other)


def irrep_row(rows_ref, first, count):
    n = count // LANES
    return jnp.concatenate([rows_ref[pl.ds(first + k, 1), :] for k in range(n)], axis=1)


def pick(cd_row, values, own_row):
    width = values.shape[1]
    blocks = width // IRREPS
    block = lax.broadcasted_iota(jnp.int32, (blocks, width), 0)
    lane_block = lax.shift_right_logical(lax.broadcasted_iota(jnp.int32, (blocks, width), 1), 3)
    slabs = [
        jnp.where((block == lane_block) & (cd_row == g), jnp.float32(1), jnp.float32(0))
        for g in range(IRREPS)
    ]
    sorter = jnp.concatenate(slabs, axis=0).astype(jnp.bfloat16)
    high, low = pieces(values)
    across = (((1,), (1,)), ((), ()))
    if width == LANES:
        both = jnp.concatenate([high, low], axis=1)
        twice = jnp.concatenate([sorter, sorter], axis=1)
        by_irrep = lax.dot_general(twice, both, across, preferred_element_type=jnp.float32)
    else:
        by_irrep = lax.dot_general(
            sorter, high, across, preferred_element_type=jnp.float32
        ) + lax.dot_general(sorter, low, across, preferred_element_type=jnp.float32)
    chosen = by_irrep[:blocks]
    for g in range(1, IRREPS):
        chosen = jnp.where(own_row == g, by_irrep[g * blocks : (g + 1) * blocks], chosen)
    return chosen


def tile(t_cols, right, column, ab_row, residual):
    high, low = pieces(t_cols.T)
    left = jnp.concatenate([high, low, high, low], axis=1)
    total = jnp.dot(left, right, preferred_element_type=jnp.float32)
    same = jnp.concatenate([column] * (ab_row.shape[1] // LANES), axis=1) == ab_row
    return residual + jnp.where(same, total, jnp.float32(0))


def ladder_kernel(
    n_pair, n_virt, parts,
    t_hbm, v_hbm, r_hbm, pi_hbm, ai_hbm, cdt_hbm, cdv_hbm,
    out_ref, t_last, right_ref, column_last, ai_ref,
    t_own, v_own, pi_ref, cdt_ref, cdv_ref, t_all, v_all, column_ref,
    load_sem, t_send, t_recv, tf_send, v_send, v_recv, vf_send,
):
    p, v = lax.axis_index("pair"), lax.axis_index("virt")
    a, b = v // 2, v % 2
    c, k = p // 2, p % 2
    n_a, n_c = n_virt // 2, n_pair // 2
    rows, t_width = t_own.shape
    ab, v_width = v_own.shape
    t_blocks, v_blocks = t_width // IRREPS, v_width // IRREPS
    blocks = t_all.shape[0]

    barrier = pltpu.get_barrier_semaphore()

    def greet(dev):
        pl.semaphore_signal(barrier, inc=1, device_id=dev, device_id_type=MESH)

    far_a = [nth_other(n_a, a, s) for s in range(n_a - 1)]
    far_c = [nth_other(n_c, c, s) for s in range(n_c - 1)]
    for o in far_a:
        greet((p, o * 2 + b))
    greet((p, a * 2 + 1 - b))
    for o in far_c:
        greet((o * 2 + k, v))
    greet((c * 2 + 1 - k, v))

    loads = [
        pltpu.make_async_copy(src, dst, load_sem.at[n])
        for n, (src, dst) in enumerate(
            [
                (t_hbm, t_own), (cdt_hbm, cdt_ref), (pi_hbm, pi_ref),
                (v_hbm, v_own), (cdv_hbm, cdv_ref), (ai_hbm, ai_ref), (r_hbm, out_ref),
            ]
        )
    ]
    for load in loads:
        load.start()

    def copy(ref, owner, count, part, span, send, recv, dev):
        at = ref.at[pl.ds(pl.multiple_of(owner * count, count), count), pl.ds(part * span, span)]
        return pltpu.make_async_remote_copy(
            src_ref=at, dst_ref=at, send_sem=send, recv_sem=recv, device_id=dev, device_id_type=MESH
        )

    t_span, v_span = rows // parts, ab // parts

    def t_copy(owner, part, send, dev):
        return copy(t_all, owner, t_blocks, part, t_span, send, t_recv.at[owner * parts + part], dev)

    def v_copy(owner, part, send, dev):
        return copy(v_all, owner, v_blocks, part, v_span, send, v_recv.at[owner * parts + part], dev)

    for load in loads[:3]:
        load.wait()
    cdt_row = irrep_row(cdt_ref, v * t_width // LANES, t_width) if t_width % LANES == 0 else cdt_ref[pl.ds(v, 1), :]
    sent = []
    for h in range(parts):
        own = irrep_row(pi_ref, h * t_span // LANES, t_span)
        t_all[pl.ds(pl.multiple_of(v * t_blocks, t_blocks), t_blocks), h * t_span : (h + 1) * t_span] = pick(
            cdt_row, t_own[h * t_span : (h + 1) * t_span, :], own
        )
        if h == 0:
            pl.semaphore_wait(barrier, n_a + n_c)
        for s in reversed(range(n_a - 1)):
            sent.append(t_copy(v, h, t_send.at[s, h], (p, far_a[s] * 2 + b)))
            sent[-1].start()
        sent.append(t_copy(v, h, t_send.at[n_a - 1, h], (p, a * 2 + 1 - b)))
        sent[-1].start()

    for load in loads[3:6]:
        load.wait()
    cdv_row = irrep_row(cdv_ref, p * v_width // LANES, v_width) if v_width % LANES == 0 else cdv_ref[pl.ds(p, 1), :]
    for h in range(parts):
        own = irrep_row(ai_ref, h * v_span // LANES, v_span)
        v_all[pl.ds(pl.multiple_of(p * v_blocks, v_blocks), v_blocks), h * v_span : (h + 1) * v_span] = pick(
            cdv_row, v_own[h * v_span : (h + 1) * v_span, :], own
        )
        for s in reversed(range(n_c - 1)):
            sent.append(v_copy(p, h, v_send.at[s, h], (far_c[s] * 2 + k, v)))
            sent[-1].start()
        sent.append(v_copy(p, h, v_send.at[n_c - 1, h], (c * 2 + 1 - k, v)))
        sent[-1].start()

    for h in range(parts):
        for s in range(n_a - 1):
            onward = t_copy(far_a[s] * 2 + b, h, tf_send.at[s, h], (p, a * 2 + 1 - b))
            onward.wait_recv()
            onward.start()
            sent.append(onward)
        for s in range(n_c - 1):
            onward = v_copy(far_c[s] * 2 + k, h, vf_send.at[s, h], (c * 2 + 1 - k, v))
            onward.wait_recv()
            onward.start()
            sent.append(onward)

    early = rows - t_span
    for m in range(rows // LANES):
        labels = jnp.broadcast_to(pi_ref[m : m + 1, :], (LANES, LANES)).T
        if m * LANES < early:
            column_ref[m * LANES : (m + 1) * LANES, :] = labels
        else:
            column_last[m * LANES - early : (m + 1) * LANES - early, :] = labels

    for h in range(parts):
        span = slice(h * v_span, (h + 1) * v_span)
        for o in range(n_c):
            v_copy(o * 2 + 1 - k, h, v_send.at[0, h], (p, v)).wait_recv()
        high, low = pieces(v_all[:, span])
        right_ref[:blocks, span] = high
        right_ref[blocks : 2 * blocks, span] = high
        right_ref[2 * blocks : 3 * blocks, span] = low
        right_ref[3 * blocks :, span] = low

    ab_row = irrep_row(ai_ref, 0, ab)
    loads[6].wait()
    for h in range(parts):
        for o in range(n_a):
            t_copy(o * 2 + 1 - b, h, t_send.at[0, h], (p, v)).wait_recv()
        if h == parts - 1:
            t_last[...] = t_all[:, early:]
            break
        for m in range(h * t_span // LANES, (h + 1) * t_span // LANES):
            at = slice(m * LANES, (m + 1) * LANES)
            out_ref[at, :] = tile(t_all[:, at], right_ref[...], column_ref[at, :], ab_row, out_ref[at, :])
    for s in sent:
        s.wait_send()


def ladder(n_pair, n_virt, t, v, residual, pi, ai, cd, cdt, cdv):
    parts = 2
    rows, t_width = t.shape
    ab, v_width = v.shape
    blocks = cd // IRREPS
    vmem, dma = pltpu.VMEM, pltpu.SemaphoreType.DMA
    n_a, n_c = n_virt // 2, n_pair // 2
    operands = (t, v, residual, pi, ai, cdt, cdv)
    return pl.pallas_call(
        functools.partial(ladder_kernel, n_pair, n_virt, parts),
        out_shape=(
            vmem((rows, ab), jnp.float32),
            vmem((blocks, rows // parts), jnp.float32),
            vmem((4 * blocks, ab), jnp.bfloat16),
            vmem((rows // parts, LANES), jnp.int32),
            vmem(ai.shape, jnp.int32),
        ),
        in_specs=[pl.BlockSpec(memory_space=pltpu.HBM)] * len(operands),
        out_specs=(pl.BlockSpec(memory_space=vmem),) * 5,
        scratch_shapes=[
            vmem((rows, t_width), jnp.float32),
            vmem((ab, v_width), jnp.float32),
            vmem(pi.shape, jnp.int32),
            vmem(cdt.shape, jnp.int32),
            vmem(cdv.shape, jnp.int32),
            vmem((blocks, rows), jnp.float32),
            vmem((blocks, ab), jnp.float32),
            vmem((rows, LANES), jnp.int32),
            dma((7,)),
            dma((n_a, parts)),
            dma((n_virt * parts,)),
            dma((max(n_a - 1, 1), parts)),
            dma((n_c, parts)),
            dma((n_pair * parts,)),
            dma((max(n_c - 1, 1), parts)),
        ],
        compiler_params=pltpu.CompilerParams(
            collective_id=0, has_side_effects=True, vmem_limit_bytes=24 * 1024 * 1024
        ),
        name="pick_gather_ladder",
    )(*[pltpu.with_memory_space_constraint(x, pltpu.HBM) for x in operands])


def finish_kernel(parts, done, t_last, right_ref, column_last, ai_ref, dst, late, sem):
    rows, ab = done.shape
    late_rows = late.shape[0]
    early = rows - late_rows
    span = early // parts
    copies = [
        pltpu.make_async_copy(done.at[pl.ds(n * span, span), :], dst.at[pl.ds(n * span, span), :], sem.at[n])
        for n in range(parts)
    ]
    for c in copies:
        c.start()
    ab_row = irrep_row(ai_ref, 0, ab)
    for m in range(late_rows // LANES):
        at = slice(m * LANES, (m + 1) * LANES)
        row = early + m * LANES
        late[at, :] = tile(t_last[:, at], right_ref[...], column_last[at, :], ab_row, done[row : row + LANES, :])
        copies.append(
            pltpu.make_async_copy(late.at[pl.ds(m * LANES, LANES), :], dst.at[pl.ds(row, LANES), :], sem.at[parts + m])
        )
        copies[-1].start()
    for c in copies:
        c.wait()


def finish(done, t_last, *others):
    parts = 4
    late_rows = t_last.shape[1]
    operands = (done, t_last, *others)
    return pl.pallas_call(
        functools.partial(finish_kernel, parts),
        out_shape=jax.ShapeDtypeStruct(done.shape, done.dtype),
        in_specs=[pl.BlockSpec(memory_space=pltpu.VMEM)] * len(operands),
        out_specs=pl.BlockSpec(memory_space=pltpu.HBM),
        scratch_shapes=[
            pltpu.VMEM((late_rows, done.shape[1]), done.dtype),
            pltpu.SemaphoreType.DMA((parts + late_rows // LANES,)),
        ],
        compiler_params=pltpu.CompilerParams(vmem_limit_bytes=8 * 1024 * 1024),
        name="finish",
    )(*[pltpu.with_memory_space_constraint(x, pltpu.VMEM) for x in operands])


def solution(mesh):
    n_pair, n_virt = mesh.shape["pair"], mesh.shape["virt"]

    def shards(amplitudes, integrals, residual_in, pair_irrep, ab_irrep, cd_irrep):
        cd = cd_irrep.shape[0]
        pi, ai = pair_irrep.reshape(-1, LANES), ab_irrep.reshape(-1, LANES)

        def cd_rows(width):
            return cd_irrep.reshape(-1, LANES if width % LANES == 0 else width)

        return finish(
            *ladder(
                n_pair, n_virt, amplitudes, integrals, residual_in, pi, ai, cd,
                cd_rows(amplitudes.shape[1]), cd_rows(integrals.shape[1]),
            )
        )

    placed = (P("pair", "virt"), P("virt", "pair"), P("pair", "virt"), P("pair"), P("virt"), P())
    return jax.shard_map(
        shards, mesh=mesh, in_specs=placed, out_specs=P("pair", "virt"), check_vma=False
    )
```

```python
import functools

import jax
import jax.numpy as jnp
from jax import lax
from jax.experimental import pallas as pl
from jax.experimental.pallas import tpu as pltpu
from jax.sharding import PartitionSpec as P

IRREPS = 8
LANES = 128
MESH = pl.DeviceIdType.MESH


def pieces(x):
    high = x.astype(jnp.bfloat16)
    low = (x - high.astype(jnp.float32)).astype(jnp.bfloat16)
    return high, low


def nth_other(n, me, step):
    flip = me // (n // 2)
    mine = me + flip * (n - 1 - 2 * me)
    other = step + (step + n - mine) // n
    return other + flip * (n - 1 - 2 * other)


def irrep_row(rows_ref, first, count):
    n = count // LANES
    return jnp.concatenate([rows_ref[pl.ds(first + k, 1), :] for k in range(n)], axis=1)


def pick(cd_row, values, own_row):
    width = values.shape[1]
    blocks = width // IRREPS
    block = lax.broadcasted_iota(jnp.int32, (blocks, width), 0)
    lane_block = lax.shift_right_logical(lax.broadcasted_iota(jnp.int32, (blocks, width), 1), 3)
    slabs = [
        jnp.where((block == lane_block) & (cd_row == g), jnp.float32(1), jnp.float32(0))
        for g in range(IRREPS)
    ]
    sorter = jnp.concatenate(slabs, axis=0).astype(jnp.bfloat16)
    high, low = pieces(values)
    across = (((1,), (1,)), ((), ()))
    if width == LANES:
        both = jnp.concatenate([high, low], axis=1)
        twice = jnp.concatenate([sorter, sorter], axis=1)
        by_irrep = lax.dot_general(twice, both, across, preferred_element_type=jnp.float32)
    else:
        by_irrep = lax.dot_general(
            sorter, high, across, preferred_element_type=jnp.float32
        ) + lax.dot_general(sorter, low, across, preferred_element_type=jnp.float32)
    chosen = by_irrep[:blocks]
    for g in range(1, IRREPS):
        chosen = jnp.where(own_row == g, by_irrep[g * blocks : (g + 1) * blocks], chosen)
    return chosen


def tile(t_cols, right, column, ab_row, residual):
    high, low = pieces(t_cols.T)
    left = jnp.concatenate([high, low, high, low], axis=1)
    total = jnp.dot(left, right, preferred_element_type=jnp.float32)
    same = jnp.concatenate([column] * (ab_row.shape[1] // LANES), axis=1) == ab_row
    return residual + jnp.where(same, total, jnp.float32(0))


def ladder_kernel(
    n_pair, n_virt, parts, v_parts,
    t_hbm, v_hbm, r_hbm, pi_hbm, ai_hbm, cdt_hbm, cdv_hbm,
    out_ref, t_last, right_ref, column_last, ai_ref,
    t_own, v_own, pi_ref, cdt_ref, cdv_ref, t_all, v_all, column_ref,
    load_sem, t_send, t_recv, tf_send, tr_send, v_send, v_recv, vf_send,
):
    p, v = lax.axis_index("pair"), lax.axis_index("virt")
    a, b = v // 2, v % 2
    c, k = p // 2, p % 2
    n_a, n_c = n_virt // 2, n_pair // 2
    rows, t_width = t_own.shape
    ab, v_width = v_own.shape
    t_blocks, v_blocks = t_width // IRREPS, v_width // IRREPS
    blocks = t_all.shape[0]

    barrier = pltpu.get_barrier_semaphore()

    def greet(dev):
        pl.semaphore_signal(barrier, inc=1, device_id=dev, device_id_type=MESH)

    upper = a // (n_a // 2)
    near, far = a + 1 - 2 * upper, a - 1 + 2 * upper
    middle = jnp.logical_and(a > 0, a < n_a - 1)
    others = [nth_other(n_a, a, s) for s in range(n_a - 1)]
    far_c = [nth_other(n_c, c, s) for s in range(n_c - 1)]
    across = (p, a * 2 + 1 - b)
    greet((p, near * 2 + b))
    greet(across)
    for o in far_c:
        greet((o * 2 + k, v))
    greet((c * 2 + 1 - k, v))

    @pl.when(middle)
    def _():
        greet((p, far * 2 + b))

    loads = [
        pltpu.make_async_copy(src, dst, load_sem.at[n])
        for n, (src, dst) in enumerate(
            [
                (t_hbm, t_own), (cdt_hbm, cdt_ref), (pi_hbm, pi_ref),
                (v_hbm, v_own), (cdv_hbm, cdv_ref), (ai_hbm, ai_ref), (r_hbm, out_ref),
            ]
        )
    ]
    for load in loads:
        load.start()

    def copy(ref, owner, count, part, span, send, recv, dev):
        at = ref.at[pl.ds(pl.multiple_of(owner * count, count), count), pl.ds(part * span, span)]
        return pltpu.make_async_remote_copy(
            src_ref=at, dst_ref=at, send_sem=send, recv_sem=recv, device_id=dev, device_id_type=MESH
        )

    t_span, v_span = rows // parts, ab // v_parts

    def t_copy(owner, part, send, dev):
        return copy(t_all, owner, t_blocks, part, t_span, send, t_recv.at[owner * parts + part], dev)

    def v_copy(owner, part, send, dev):
        return copy(v_all, owner, v_blocks, part, v_span, send, v_recv.at[owner * v_parts + part], dev)

    for load in loads[:3]:
        load.wait()
    cdt_row = irrep_row(cdt_ref, v * t_width // LANES, t_width) if t_width % LANES == 0 else cdt_ref[pl.ds(v, 1), :]
    sent, relayed = [], []
    for h in range(parts):
        own = irrep_row(pi_ref, h * t_span // LANES, t_span)
        t_all[pl.ds(pl.multiple_of(v * t_blocks, t_blocks), t_blocks), h * t_span : (h + 1) * t_span] = pick(
            cdt_row, t_own[h * t_span : (h + 1) * t_span, :], own
        )
        if h == 0:
            pl.semaphore_wait(barrier, n_c + 2 + middle.astype(jnp.int32))
        sent.append(t_copy(v, h, t_send.at[0, h], across))
        sent[-1].start()
        sent.append(t_copy(v, h, t_send.at[1, h], (p, near * 2 + b)))
        sent[-1].start()
        relayed.append(t_copy(v, h, t_send.at[2, h], (p, far * 2 + b)))
        pl.when(middle)(relayed[-1].start)

    for load in loads[3:6]:
        load.wait()
    cdv_row = irrep_row(cdv_ref, p * v_width // LANES, v_width) if v_width % LANES == 0 else cdv_ref[pl.ds(p, 1), :]
    for h in range(v_parts):
        own = irrep_row(ai_ref, h * v_span // LANES, v_span)
        v_all[pl.ds(pl.multiple_of(p * v_blocks, v_blocks), v_blocks), h * v_span : (h + 1) * v_span] = pick(
            cdv_row, v_own[h * v_span : (h + 1) * v_span, :], own
        )
        for s in reversed(range(n_c - 1)):
            sent.append(v_copy(p, h, v_send.at[s, h], (far_c[s] * 2 + k, v)))
            sent[-1].start()
        sent.append(v_copy(p, h, v_send.at[n_c - 1, h], (c * 2 + 1 - k, v)))
        sent[-1].start()

    def pass_v(h):
        for s in range(n_c - 1):
            onward = v_copy(far_c[s] * 2 + k, h, vf_send.at[s, h], (c * 2 + 1 - k, v))
            onward.wait_recv()
            onward.start()
            sent.append(onward)

    order = sorted((h + s, s, h) for h in range(parts) for s in range(n_a - 1))
    for n, (_, s, h) in enumerate(order):
        source = others[s]
        onward = t_copy(source * 2 + b, h, tf_send.at[s, h], across)
        onward.wait_recv()
        beyond = a - 1 + 2 * ((a - source + n_a) // n_a)
        relayed.append(t_copy(source * 2 + b, h, tr_send.at[s, h], (p, beyond * 2 + b)))
        pl.when(middle)(relayed[-1].start)
        onward.start()
        sent.append(onward)
        if n == 2 * len(order) // 3:
            pass_v(0)
    for h in range(1, v_parts):
        pass_v(h)

    early = rows - t_last.shape[1]
    for m in range(rows // LANES):
        labels = jnp.broadcast_to(pi_ref[m : m + 1, :], (LANES, LANES)).T
        if m * LANES < early:
            column_ref[m * LANES : (m + 1) * LANES, :] = labels
        else:
            column_last[m * LANES - early : (m + 1) * LANES - early, :] = labels

    for h in range(v_parts):
        span = slice(h * v_span, (h + 1) * v_span)
        for o in range(n_c):
            v_copy(o * 2 + 1 - k, h, v_send.at[0, h], (p, v)).wait_recv()
        high, low = pieces(v_all[:, span])
        right_ref[:blocks, span] = high
        right_ref[blocks : 2 * blocks, span] = high
        right_ref[2 * blocks : 3 * blocks, span] = low
        right_ref[3 * blocks :, span] = low

    ab_row = irrep_row(ai_ref, 0, ab)
    loads[6].wait()
    for h in range(parts):
        for o in range(n_a):
            t_copy(o * 2 + 1 - b, h, t_send.at[0, h], (p, v)).wait_recv()
        if h * t_span >= early:
            t_last[:, h * t_span - early : (h + 1) * t_span - early] = t_all[:, h * t_span : (h + 1) * t_span]
            continue
        for m in range(h * t_span // LANES, (h + 1) * t_span // LANES):
            at = slice(m * LANES, (m + 1) * LANES)
            out_ref[at, :] = tile(t_all[:, at], right_ref[...], column_ref[at, :], ab_row, out_ref[at, :])
    for s in sent:
        s.wait_send()

    @pl.when(middle)
    def _():
        for s in relayed:
            s.wait_send()


def ladder(n_pair, n_virt, t, v, residual, pi, ai, cd, cdt, cdv):
    parts, v_parts = 4, 2
    rows, t_width = t.shape
    ab, v_width = v.shape
    blocks = cd // IRREPS
    vmem, dma = pltpu.VMEM, pltpu.SemaphoreType.DMA
    n_a, n_c = n_virt // 2, n_pair // 2
    operands = (t, v, residual, pi, ai, cdt, cdv)
    return pl.pallas_call(
        functools.partial(ladder_kernel, n_pair, n_virt, parts, v_parts),
        out_shape=(
            vmem((rows, ab), jnp.float32),
            vmem((blocks, rows // 2), jnp.float32),
            vmem((4 * blocks, ab), jnp.bfloat16),
            vmem((rows // 2, LANES), jnp.int32),
            vmem(ai.shape, jnp.int32),
        ),
        in_specs=[pl.BlockSpec(memory_space=pltpu.HBM)] * len(operands),
        out_specs=(pl.BlockSpec(memory_space=vmem),) * 5,
        scratch_shapes=[
            vmem((rows, t_width), jnp.float32),
            vmem((ab, v_width), jnp.float32),
            vmem(pi.shape, jnp.int32),
            vmem(cdt.shape, jnp.int32),
            vmem(cdv.shape, jnp.int32),
            vmem((blocks, rows), jnp.float32),
            vmem((blocks, ab), jnp.float32),
            vmem((rows, LANES), jnp.int32),
            dma((7,)),
            dma((3, parts)),
            dma((n_virt * parts,)),
            dma((max(n_a - 1, 1), parts)),
            dma((max(n_a - 1, 1), parts)),
            dma((n_c, v_parts)),
            dma((n_pair * v_parts,)),
            dma((max(n_c - 1, 1), v_parts)),
        ],
        compiler_params=pltpu.CompilerParams(
            collective_id=0, has_side_effects=True, vmem_limit_bytes=24 * 1024 * 1024
        ),
        name="pick_gather_ladder",
    )(*[pltpu.with_memory_space_constraint(x, pltpu.HBM) for x in operands])


def finish_kernel(parts, done, t_last, right_ref, column_last, ai_ref, dst, late, sem):
    rows, ab = done.shape
    late_rows = late.shape[0]
    early = rows - late_rows
    span = early // parts
    copies = [
        pltpu.make_async_copy(done.at[pl.ds(n * span, span), :], dst.at[pl.ds(n * span, span), :], sem.at[n])
        for n in range(parts)
    ]
    for c in copies:
        c.start()
    ab_row = irrep_row(ai_ref, 0, ab)
    for m in range(late_rows // LANES):
        at = slice(m * LANES, (m + 1) * LANES)
        row = early + m * LANES
        late[at, :] = tile(t_last[:, at], right_ref[...], column_last[at, :], ab_row, done[row : row + LANES, :])
        copies.append(
            pltpu.make_async_copy(late.at[pl.ds(m * LANES, LANES), :], dst.at[pl.ds(row, LANES), :], sem.at[parts + m])
        )
        copies[-1].start()
    for c in copies:
        c.wait()


def finish(done, t_last, *others):
    parts = 4
    late_rows = t_last.shape[1]
    operands = (done, t_last, *others)
    return pl.pallas_call(
        functools.partial(finish_kernel, parts),
        out_shape=jax.ShapeDtypeStruct(done.shape, done.dtype),
        in_specs=[pl.BlockSpec(memory_space=pltpu.VMEM)] * len(operands),
        out_specs=pl.BlockSpec(memory_space=pltpu.HBM),
        scratch_shapes=[
            pltpu.VMEM((late_rows, done.shape[1]), done.dtype),
            pltpu.SemaphoreType.DMA((parts + late_rows // LANES,)),
        ],
        compiler_params=pltpu.CompilerParams(vmem_limit_bytes=8 * 1024 * 1024),
        name="finish",
    )(*[pltpu.with_memory_space_constraint(x, pltpu.VMEM) for x in operands])


def solution(mesh):
    n_pair, n_virt = mesh.shape["pair"], mesh.shape["virt"]

    def shards(amplitudes, integrals, residual_in, pair_irrep, ab_irrep, cd_irrep):
        cd = cd_irrep.shape[0]
        pi, ai = pair_irrep.reshape(-1, LANES), ab_irrep.reshape(-1, LANES)

        def cd_rows(width):
            return cd_irrep.reshape(-1, LANES if width % LANES == 0 else width)

        return finish(
            *ladder(
                n_pair, n_virt, amplitudes, integrals, residual_in, pi, ai, cd,
                cd_rows(amplitudes.shape[1]), cd_rows(integrals.shape[1]),
            )
        )

    placed = (P("pair", "virt"), P("virt", "pair"), P("pair", "virt"), P("pair"), P("virt"), P())
    return jax.shard_map(
        shards, mesh=mesh, in_specs=placed, out_specs=P("pair", "virt"), check_vma=False
    )
```

```python
import functools

import jax
import jax.numpy as jnp
from jax import lax
from jax.experimental import pallas as pl
from jax.experimental.pallas import tpu as pltpu
from jax.sharding import PartitionSpec as P

IRREPS = 8
LANES = 128
MESH = pl.DeviceIdType.MESH


def pieces(x):
    high = x.astype(jnp.bfloat16)
    low = (x - high.astype(jnp.float32)).astype(jnp.bfloat16)
    return high, low


def irrep_row(rows_ref, first, count):
    n = count // LANES
    return jnp.concatenate([rows_ref[pl.ds(first + k, 1), :] for k in range(n)], axis=1)


def pick(cd_row, values, own_row):
    width = values.shape[1]
    blocks = width // IRREPS
    block = lax.broadcasted_iota(jnp.int32, (blocks, width), 0)
    lane_block = lax.shift_right_logical(lax.broadcasted_iota(jnp.int32, (blocks, width), 1), 3)
    slabs = [
        jnp.where((block == lane_block) & (cd_row == g), jnp.float32(1), jnp.float32(0))
        for g in range(IRREPS)
    ]
    sorter = jnp.concatenate(slabs, axis=0).astype(jnp.bfloat16)
    high, low = pieces(values)
    across = (((1,), (1,)), ((), ()))
    if width == LANES:
        both = jnp.concatenate([high, low], axis=1)
        twice = jnp.concatenate([sorter, sorter], axis=1)
        by_irrep = lax.dot_general(twice, both, across, preferred_element_type=jnp.float32)
    else:
        by_irrep = lax.dot_general(
            sorter, high, across, preferred_element_type=jnp.float32
        ) + lax.dot_general(sorter, low, across, preferred_element_type=jnp.float32)
    chosen = by_irrep[:blocks]
    for g in range(1, IRREPS):
        chosen = jnp.where(own_row == g, by_irrep[g * blocks : (g + 1) * blocks], chosen)
    return chosen


def tile(t_cols, right, column, ab_row, residual):
    high, low = pieces(t_cols.T)
    left = jnp.concatenate([high, low, high, low], axis=1)
    total = jnp.dot(left, right, preferred_element_type=jnp.float32)
    same = jnp.concatenate([column] * (ab_row.shape[1] // LANES), axis=1) == ab_row
    return residual + jnp.where(same, total, jnp.float32(0))


def ladder_kernel(
    n_pair, n_virt, parts,
    t_hbm, v_hbm, r_hbm, pi_hbm, ai_hbm, cdt_hbm, cdv_hbm,
    out_ref, t_last, right_ref, column_last, ai_ref,
    t_own, v_own, pi_ref, cdt_ref, cdv_ref, t_all, v_all, column_ref,
    load_sem, t_send, t_recv, v_send, v_recv,
):
    p, v = lax.axis_index("pair"), lax.axis_index("virt")
    rows, t_width = t_own.shape
    ab, v_width = v_own.shape
    t_blocks, v_blocks = t_width // IRREPS, v_width // IRREPS
    blocks = t_all.shape[0]

    barrier = pltpu.get_barrier_semaphore()

    def greet(dev):
        pl.semaphore_signal(barrier, inc=1, device_id=dev, device_id_type=MESH)

    t_peers = [(p, lax.rem(v + s, n_virt)) for s in range(1, n_virt)]
    v_peers = [(lax.rem(p + s, n_pair), v) for s in range(1, n_pair)]
    for dev in t_peers + v_peers:
        greet(dev)

    loads = [
        pltpu.make_async_copy(src, dst, load_sem.at[n])
        for n, (src, dst) in enumerate(
            [
                (t_hbm, t_own), (cdt_hbm, cdt_ref), (pi_hbm, pi_ref),
                (v_hbm, v_own), (cdv_hbm, cdv_ref), (ai_hbm, ai_ref), (r_hbm, out_ref),
            ]
        )
    ]
    for load in loads:
        load.start()

    def copy(ref, owner, count, part, span, send, recv, dev):
        at = ref.at[pl.ds(pl.multiple_of(owner * count, count), count), pl.ds(part * span, span)]
        return pltpu.make_async_remote_copy(
            src_ref=at, dst_ref=at, send_sem=send, recv_sem=recv, device_id=dev, device_id_type=MESH
        )

    t_span, v_span = rows // parts, ab // parts

    def t_copy(owner, part, send, dev):
        return copy(t_all, owner, t_blocks, part, t_span, send, t_recv.at[owner * parts + part], dev)

    def v_copy(owner, part, send, dev):
        return copy(v_all, owner, v_blocks, part, v_span, send, v_recv.at[owner * parts + part], dev)

    for load in loads[:3]:
        load.wait()
    cdt_row = irrep_row(cdt_ref, v * t_width // LANES, t_width) if t_width % LANES == 0 else cdt_ref[pl.ds(v, 1), :]
    sent = []
    for h in range(parts):
        own = irrep_row(pi_ref, h * t_span // LANES, t_span)
        t_all[pl.ds(pl.multiple_of(v * t_blocks, t_blocks), t_blocks), h * t_span : (h + 1) * t_span] = pick(
            cdt_row, t_own[h * t_span : (h + 1) * t_span, :], own
        )
        if h == 0:
            pl.semaphore_wait(barrier, n_virt + n_pair - 2)
        for s, dev in enumerate(t_peers):
            sent.append(t_copy(v, h, t_send.at[s, h], dev))
            sent[-1].start()

    for load in loads[3:6]:
        load.wait()
    cdv_row = irrep_row(cdv_ref, p * v_width // LANES, v_width) if v_width % LANES == 0 else cdv_ref[pl.ds(p, 1), :]
    for h in range(parts):
        own = irrep_row(ai_ref, h * v_span // LANES, v_span)
        v_all[pl.ds(pl.multiple_of(p * v_blocks, v_blocks), v_blocks), h * v_span : (h + 1) * v_span] = pick(
            cdv_row, v_own[h * v_span : (h + 1) * v_span, :], own
        )
        for s, dev in enumerate(v_peers):
            sent.append(v_copy(p, h, v_send.at[s, h], dev))
            sent[-1].start()

    early = rows - t_span
    for m in range(rows // LANES):
        labels = jnp.broadcast_to(pi_ref[m : m + 1, :], (LANES, LANES)).T
        if m * LANES < early:
            column_ref[m * LANES : (m + 1) * LANES, :] = labels
        else:
            column_last[m * LANES - early : (m + 1) * LANES - early, :] = labels

    for h in range(parts):
        span = slice(h * v_span, (h + 1) * v_span)
        for owner, _ in v_peers:
            v_copy(owner, h, v_send.at[0, h], (p, v)).wait_recv()
        high, low = pieces(v_all[:, span])
        right_ref[:blocks, span] = high
        right_ref[blocks : 2 * blocks, span] = high
        right_ref[2 * blocks : 3 * blocks, span] = low
        right_ref[3 * blocks :, span] = low

    ab_row = irrep_row(ai_ref, 0, ab)
    loads[6].wait()
    for h in range(parts):
        for _, owner in t_peers:
            t_copy(owner, h, t_send.at[0, h], (p, v)).wait_recv()
        if h == parts - 1:
            t_last[...] = t_all[:, early:]
            break
        for m in range(h * t_span // LANES, (h + 1) * t_span // LANES):
            at = slice(m * LANES, (m + 1) * LANES)
            out_ref[at, :] = tile(t_all[:, at], right_ref[...], column_ref[at, :], ab_row, out_ref[at, :])
    for s in sent:
        s.wait_send()


def ladder(n_pair, n_virt, t, v, residual, pi, ai, cd, cdt, cdv):
    parts = 2
    rows, t_width = t.shape
    ab, v_width = v.shape
    blocks = cd // IRREPS
    vmem, dma = pltpu.VMEM, pltpu.SemaphoreType.DMA
    operands = (t, v, residual, pi, ai, cdt, cdv)
    return pl.pallas_call(
        functools.partial(ladder_kernel, n_pair, n_virt, parts),
        out_shape=(
            vmem((rows, ab), jnp.float32),
            vmem((blocks, rows // parts), jnp.float32),
            vmem((4 * blocks, ab), jnp.bfloat16),
            vmem((rows // parts, LANES), jnp.int32),
            vmem(ai.shape, jnp.int32),
        ),
        in_specs=[pl.BlockSpec(memory_space=pltpu.HBM)] * len(operands),
        out_specs=(pl.BlockSpec(memory_space=vmem),) * 5,
        scratch_shapes=[
            vmem((rows, t_width), jnp.float32),
            vmem((ab, v_width), jnp.float32),
            vmem(pi.shape, jnp.int32),
            vmem(cdt.shape, jnp.int32),
            vmem(cdv.shape, jnp.int32),
            vmem((blocks, rows), jnp.float32),
            vmem((blocks, ab), jnp.float32),
            vmem((rows, LANES), jnp.int32),
            dma((7,)),
            dma((n_virt - 1, parts)),
            dma((n_virt * parts,)),
            dma((n_pair - 1, parts)),
            dma((n_pair * parts,)),
        ],
        compiler_params=pltpu.CompilerParams(
            collective_id=0, has_side_effects=True, vmem_limit_bytes=24 * 1024 * 1024
        ),
        name="pick_gather_ladder",
    )(*[pltpu.with_memory_space_constraint(x, pltpu.HBM) for x in operands])


def finish_kernel(parts, done, t_last, right_ref, column_last, ai_ref, dst, late, sem):
    rows, ab = done.shape
    late_rows = late.shape[0]
    early = rows - late_rows
    span = early // parts
    copies = [
        pltpu.make_async_copy(done.at[pl.ds(n * span, span), :], dst.at[pl.ds(n * span, span), :], sem.at[n])
        for n in range(parts)
    ]
    for c in copies:
        c.start()
    ab_row = irrep_row(ai_ref, 0, ab)
    for m in range(late_rows // LANES):
        at = slice(m * LANES, (m + 1) * LANES)
        row = early + m * LANES
        late[at, :] = tile(t_last[:, at], right_ref[...], column_last[at, :], ab_row, done[row : row + LANES, :])
        copies.append(
            pltpu.make_async_copy(late.at[pl.ds(m * LANES, LANES), :], dst.at[pl.ds(row, LANES), :], sem.at[parts + m])
        )
        copies[-1].start()
    for c in copies:
        c.wait()


def finish(done, t_last, *others):
    parts = 4
    late_rows = t_last.shape[1]
    operands = (done, t_last, *others)
    return pl.pallas_call(
        functools.partial(finish_kernel, parts),
        out_shape=jax.ShapeDtypeStruct(done.shape, done.dtype),
        in_specs=[pl.BlockSpec(memory_space=pltpu.VMEM)] * len(operands),
        out_specs=pl.BlockSpec(memory_space=pltpu.HBM),
        scratch_shapes=[
            pltpu.VMEM((late_rows, done.shape[1]), done.dtype),
            pltpu.SemaphoreType.DMA((parts + late_rows // LANES,)),
        ],
        compiler_params=pltpu.CompilerParams(vmem_limit_bytes=8 * 1024 * 1024),
        name="finish",
    )(*[pltpu.with_memory_space_constraint(x, pltpu.VMEM) for x in operands])


def solution(mesh):
    n_pair, n_virt = mesh.shape["pair"], mesh.shape["virt"]

    def shards(amplitudes, integrals, residual_in, pair_irrep, ab_irrep, cd_irrep):
        cd = cd_irrep.shape[0]
        pi, ai = pair_irrep.reshape(-1, LANES), ab_irrep.reshape(-1, LANES)

        def cd_rows(width):
            return cd_irrep.reshape(-1, LANES if width % LANES == 0 else width)

        return finish(
            *ladder(
                n_pair, n_virt, amplitudes, integrals, residual_in, pi, ai, cd,
                cd_rows(amplitudes.shape[1]), cd_rows(integrals.shape[1]),
            )
        )

    placed = (P("pair", "virt"), P("virt", "pair"), P("pair", "virt"), P("pair"), P("virt"), P())
    return jax.shard_map(
        shards, mesh=mesh, in_specs=placed, out_specs=P("pair", "virt"), check_vma=False
    )
```

```python
import functools

import jax
import jax.numpy as jnp
from jax import lax
from jax.experimental import pallas as pl
from jax.experimental.pallas import tpu as pltpu
from jax.sharding import PartitionSpec as P

IRREPS = 8
LANES = 128
MESH = pl.DeviceIdType.MESH


def pieces(x):
    high = x.astype(jnp.bfloat16)
    low = (x - high.astype(jnp.float32)).astype(jnp.bfloat16)
    return high, low


def nth_other(n, me, step):
    flip = me // (n // 2)
    mine = me + flip * (n - 1 - 2 * me)
    other = step + (step + n - mine) // n
    return other + flip * (n - 1 - 2 * other)


def irrep_row(rows_ref, first, count):
    n = count // LANES
    return jnp.concatenate([rows_ref[pl.ds(first + k, 1), :] for k in range(n)], axis=1)


def pick(cd_row, values, own_row):
    width = values.shape[1]
    blocks = width // IRREPS
    block = lax.broadcasted_iota(jnp.int32, (blocks, width), 0)
    lane_block = lax.shift_right_logical(lax.broadcasted_iota(jnp.int32, (blocks, width), 1), 3)
    slabs = [
        jnp.where((block == lane_block) & (cd_row == g), jnp.float32(1), jnp.float32(0))
        for g in range(IRREPS)
    ]
    sorter = jnp.concatenate(slabs, axis=0).astype(jnp.bfloat16)
    high, low = pieces(values)
    across = (((1,), (1,)), ((), ()))
    if width == LANES:
        both = jnp.concatenate([high, low], axis=1)
        twice = jnp.concatenate([sorter, sorter], axis=1)
        by_irrep = lax.dot_general(twice, both, across, preferred_element_type=jnp.float32)
    else:
        by_irrep = lax.dot_general(
            sorter, high, across, preferred_element_type=jnp.float32
        ) + lax.dot_general(sorter, low, across, preferred_element_type=jnp.float32)
    chosen = by_irrep[:blocks]
    for g in range(1, IRREPS):
        chosen = jnp.where(own_row == g, by_irrep[g * blocks : (g + 1) * blocks], chosen)
    return chosen


def tile(t_cols, right, column, ab_row, residual):
    high, low = pieces(t_cols.T)
    left = jnp.concatenate([high, low, high, low], axis=1)
    total = jnp.dot(left, right, preferred_element_type=jnp.float32)
    same = jnp.concatenate([column] * (ab_row.shape[1] // LANES), axis=1) == ab_row
    return residual + jnp.where(same, total, jnp.float32(0))


def ladder_kernel(
    n_pair, n_virt, parts, v_parts,
    t_hbm, v_hbm, r_hbm, pi_hbm, ai_hbm, cdt_hbm, cdv_hbm,
    out_ref, t_last, right_ref, column_last, ai_ref,
    t_own, v_own, pi_ref, cdt_ref, cdv_ref, t_all, v_all, column_ref,
    load_sem, t_send, t_recv, tf_send, v_send, v_recv, vf_send,
):
    p, v = lax.axis_index("pair"), lax.axis_index("virt")
    a, b = v // 2, v % 2
    c, k = p // 2, p % 2
    n_a, n_c = n_virt // 2, n_pair // 2
    rows, t_width = t_own.shape
    ab, v_width = v_own.shape
    t_blocks, v_blocks = t_width // IRREPS, v_width // IRREPS
    blocks = t_all.shape[0]

    barrier = pltpu.get_barrier_semaphore()

    def greet(dev):
        pl.semaphore_signal(barrier, inc=1, device_id=dev, device_id_type=MESH)

    far_a = [nth_other(n_a, a, s) for s in range(n_a - 1)]
    far_c = [nth_other(n_c, c, s) for s in range(n_c - 1)]
    for o in far_a:
        greet((p, o * 2 + b))
    greet((p, a * 2 + 1 - b))
    for o in far_c:
        greet((o * 2 + k, v))
    greet((c * 2 + 1 - k, v))

    t_span, v_span = rows // parts, ab // v_parts

    def load(src, dst, n):
        copy = pltpu.make_async_copy(src, dst, load_sem.at[n])
        copy.start()
        return copy

    labels = [load(cdt_hbm, cdt_ref, 0), load(pi_hbm, pi_ref, 1)]
    t_loads = [
        load(t_hbm.at[pl.ds(h * t_span, t_span), :], t_own.at[pl.ds(h * t_span, t_span), :], 5 + h)
        for h in range(parts)
    ]
    v_loads = [load(cdv_hbm, cdv_ref, 2), load(ai_hbm, ai_ref, 3), load(v_hbm, v_own, 4)]

    def copy(ref, owner, count, part, span, send, recv, dev):
        at = ref.at[pl.ds(pl.multiple_of(owner * count, count), count), pl.ds(part * span, span)]
        return pltpu.make_async_remote_copy(
            src_ref=at, dst_ref=at, send_sem=send, recv_sem=recv, device_id=dev, device_id_type=MESH
        )

    def t_copy(owner, part, send, dev):
        return copy(t_all, owner, t_blocks, part, t_span, send, t_recv.at[owner * parts + part], dev)

    def v_copy(owner, part, send, dev):
        return copy(v_all, owner, v_blocks, part, v_span, send, v_recv.at[owner * v_parts + part], dev)

    def send_t(h):
        mine = [t_copy(v, h, t_send.at[s, h], (p, far_a[s] * 2 + b)) for s in reversed(range(n_a - 1))]
        beside = t_copy(v, h, t_send.at[n_a - 1, h], (p, a * 2 + 1 - b))
        for one in [*mine, beside]:
            one.start()
        sent.append(beside)
        return mine

    def pass_t(h, steps):
        for s in steps:
            onward = t_copy(far_a[s] * 2 + b, h, tf_send.at[s, h], (p, a * 2 + 1 - b))
            onward.wait_recv()
            onward.start()
            sent.append(onward)

    def pass_v(h):
        for s in range(n_c - 1):
            onward = v_copy(far_c[s] * 2 + k, h, vf_send.at[s, h], (c * 2 + 1 - k, v))
            onward.wait_recv()
            onward.start()
            sent.append(onward)

    for one in labels:
        one.wait()
    cdt_row = irrep_row(cdt_ref, v * t_width // LANES, t_width) if t_width % LANES == 0 else cdt_ref[pl.ds(v, 1), :]
    sent, flying = [], []
    for h in range(parts):
        t_loads[h].wait()
        own = irrep_row(pi_ref, h * t_span // LANES, t_span)
        t_all[pl.ds(pl.multiple_of(v * t_blocks, t_blocks), t_blocks), h * t_span : (h + 1) * t_span] = pick(
            cdt_row, t_own[h * t_span : (h + 1) * t_span, :], own
        )
        if h == 0:
            pl.semaphore_wait(barrier, n_a + n_c)
        if h < 2:
            flying.append(send_t(h))

    for one in v_loads:
        one.wait()
    load_r = load(r_hbm, out_ref, 5 + parts)
    cdv_row = irrep_row(cdv_ref, p * v_width // LANES, v_width) if v_width % LANES == 0 else cdv_ref[pl.ds(p, 1), :]
    for h in range(v_parts):
        own = irrep_row(ai_ref, h * v_span // LANES, v_span)
        v_all[pl.ds(pl.multiple_of(p * v_blocks, v_blocks), v_blocks), h * v_span : (h + 1) * v_span] = pick(
            cdv_row, v_own[h * v_span : (h + 1) * v_span, :], own
        )
        for s in reversed(range(n_c - 1)):
            sent.append(v_copy(p, h, v_send.at[s, h], (far_c[s] * 2 + k, v)))
            sent[-1].start()
        sent.append(v_copy(p, h, v_send.at[n_c - 1, h], (c * 2 + 1 - k, v)))
        sent[-1].start()

    for h in range(parts):
        pass_t(h, range(1))
        if h + 2 < parts:
            for one in flying[h]:
                one.wait_send()
            flying.append(send_t(h + 2))
        else:
            sent.extend(flying[h])
        pass_t(h, range(1, n_a - 1))
        if h % 2 == 1:
            pass_v(h // 2)

    early = rows - t_last.shape[1]
    for m in range(rows // LANES):
        labels = jnp.broadcast_to(pi_ref[m : m + 1, :], (LANES, LANES)).T
        if m * LANES < early:
            column_ref[m * LANES : (m + 1) * LANES, :] = labels
        else:
            column_last[m * LANES - early : (m + 1) * LANES - early, :] = labels

    for h in range(v_parts):
        span = slice(h * v_span, (h + 1) * v_span)
        for o in range(n_c):
            v_copy(o * 2 + 1 - k, h, v_send.at[0, h], (p, v)).wait_recv()
        high, low = pieces(v_all[:, span])
        right_ref[:blocks, span] = high
        right_ref[blocks : 2 * blocks, span] = high
        right_ref[2 * blocks : 3 * blocks, span] = low
        right_ref[3 * blocks :, span] = low

    ab_row = irrep_row(ai_ref, 0, ab)
    load_r.wait()
    for h in range(parts):
        for o in range(n_a):
            t_copy(o * 2 + 1 - b, h, t_send.at[0, h], (p, v)).wait_recv()
        if h * t_span >= early:
            t_last[:, h * t_span - early : (h + 1) * t_span - early] = t_all[:, h * t_span : (h + 1) * t_span]
            continue
        for m in range(h * t_span // LANES, (h + 1) * t_span // LANES):
            at = slice(m * LANES, (m + 1) * LANES)
            out_ref[at, :] = tile(t_all[:, at], right_ref[...], column_ref[at, :], ab_row, out_ref[at, :])
    for s in sent:
        s.wait_send()


def ladder(n_pair, n_virt, t, v, residual, pi, ai, cd, cdt, cdv):
    parts, v_parts = 4, 2
    rows, t_width = t.shape
    ab, v_width = v.shape
    blocks = cd // IRREPS
    vmem, dma = pltpu.VMEM, pltpu.SemaphoreType.DMA
    n_a, n_c = n_virt // 2, n_pair // 2
    operands = (t, v, residual, pi, ai, cdt, cdv)
    return pl.pallas_call(
        functools.partial(ladder_kernel, n_pair, n_virt, parts, v_parts),
        out_shape=(
            vmem((rows, ab), jnp.float32),
            vmem((blocks, rows // 2), jnp.float32),
            vmem((4 * blocks, ab), jnp.bfloat16),
            vmem((rows // 2, LANES), jnp.int32),
            vmem(ai.shape, jnp.int32),
        ),
        in_specs=[pl.BlockSpec(memory_space=pltpu.HBM)] * len(operands),
        out_specs=(pl.BlockSpec(memory_space=vmem),) * 5,
        scratch_shapes=[
            vmem((rows, t_width), jnp.float32),
            vmem((ab, v_width), jnp.float32),
            vmem(pi.shape, jnp.int32),
            vmem(cdt.shape, jnp.int32),
            vmem(cdv.shape, jnp.int32),
            vmem((blocks, rows), jnp.float32),
            vmem((blocks, ab), jnp.float32),
            vmem((rows, LANES), jnp.int32),
            dma((6 + parts,)),
            dma((n_a, parts)),
            dma((n_virt * parts,)),
            dma((max(n_a - 1, 1), parts)),
            dma((n_c, v_parts)),
            dma((n_pair * v_parts,)),
            dma((max(n_c - 1, 1), v_parts)),
        ],
        compiler_params=pltpu.CompilerParams(
            collective_id=0, has_side_effects=True, vmem_limit_bytes=24 * 1024 * 1024
        ),
        name="pick_gather_ladder",
    )(*[pltpu.with_memory_space_constraint(x, pltpu.HBM) for x in operands])


def finish_kernel(parts, done, t_last, right_ref, column_last, ai_ref, dst, late, sem):
    rows, ab = done.shape
    late_rows = late.shape[0]
    early = rows - late_rows
    span = early // parts
    copies = [
        pltpu.make_async_copy(done.at[pl.ds(n * span, span), :], dst.at[pl.ds(n * span, span), :], sem.at[n])
        for n in range(parts)
    ]
    for c in copies:
        c.start()
    ab_row = irrep_row(ai_ref, 0, ab)
    for m in range(late_rows // LANES):
        at = slice(m * LANES, (m + 1) * LANES)
        row = early + m * LANES
        late[at, :] = tile(t_last[:, at], right_ref[...], column_last[at, :], ab_row, done[row : row + LANES, :])
        copies.append(
            pltpu.make_async_copy(late.at[pl.ds(m * LANES, LANES), :], dst.at[pl.ds(row, LANES), :], sem.at[parts + m])
        )
        copies[-1].start()
    for c in copies:
        c.wait()


def finish(done, t_last, *others):
    parts = 4
    late_rows = t_last.shape[1]
    operands = (done, t_last, *others)
    return pl.pallas_call(
        functools.partial(finish_kernel, parts),
        out_shape=jax.ShapeDtypeStruct(done.shape, done.dtype),
        in_specs=[pl.BlockSpec(memory_space=pltpu.VMEM)] * len(operands),
        out_specs=pl.BlockSpec(memory_space=pltpu.HBM),
        scratch_shapes=[
            pltpu.VMEM((late_rows, done.shape[1]), done.dtype),
            pltpu.SemaphoreType.DMA((parts + late_rows // LANES,)),
        ],
        compiler_params=pltpu.CompilerParams(vmem_limit_bytes=8 * 1024 * 1024),
        name="finish",
    )(*[pltpu.with_memory_space_constraint(x, pltpu.VMEM) for x in operands])


def solution(mesh):
    n_pair, n_virt = mesh.shape["pair"], mesh.shape["virt"]

    def shards(amplitudes, integrals, residual_in, pair_irrep, ab_irrep, cd_irrep):
        cd = cd_irrep.shape[0]
        pi, ai = pair_irrep.reshape(-1, LANES), ab_irrep.reshape(-1, LANES)

        def cd_rows(width):
            return cd_irrep.reshape(-1, LANES if width % LANES == 0 else width)

        return finish(
            *ladder(
                n_pair, n_virt, amplitudes, integrals, residual_in, pi, ai, cd,
                cd_rows(amplitudes.shape[1]), cd_rows(integrals.shape[1]),
            )
        )

    placed = (P("pair", "virt"), P("virt", "pair"), P("pair", "virt"), P("pair"), P("virt"), P())
    return jax.shard_map(
        shards, mesh=mesh, in_specs=placed, out_specs=P("pair", "virt"), check_vma=False
    )
```

```python
import functools

import jax
import jax.numpy as jnp
from jax import lax
from jax.experimental import pallas as pl
from jax.experimental.pallas import tpu as pltpu
from jax.sharding import PartitionSpec as P

IRREPS = 8
LANES = 128
MESH = pl.DeviceIdType.MESH


def pieces(x):
    high = x.astype(jnp.bfloat16)
    low = (x - high.astype(jnp.float32)).astype(jnp.bfloat16)
    return high, low


def nth_other(n, me, step):
    flip = me // (n // 2)
    mine = me + flip * (n - 1 - 2 * me)
    other = step + (step + n - mine) // n
    return other + flip * (n - 1 - 2 * other)


def irrep_row(rows_ref, first, count):
    n = count // LANES
    return jnp.concatenate([rows_ref[pl.ds(first + k, 1), :] for k in range(n)], axis=1)


def pick(cd_row, values, own_row):
    width = values.shape[1]
    blocks = width // IRREPS
    block = lax.broadcasted_iota(jnp.int32, (blocks, width), 0)
    lane_block = lax.shift_right_logical(lax.broadcasted_iota(jnp.int32, (blocks, width), 1), 3)
    slabs = [
        jnp.where((block == lane_block) & (cd_row == g), jnp.float32(1), jnp.float32(0))
        for g in range(IRREPS)
    ]
    sorter = jnp.concatenate(slabs, axis=0).astype(jnp.bfloat16)
    high, low = pieces(values)
    across = (((1,), (1,)), ((), ()))
    if width == LANES:
        both = jnp.concatenate([high, low], axis=1)
        twice = jnp.concatenate([sorter, sorter], axis=1)
        by_irrep = lax.dot_general(twice, both, across, preferred_element_type=jnp.float32)
    else:
        by_irrep = lax.dot_general(
            sorter, high, across, preferred_element_type=jnp.float32
        ) + lax.dot_general(sorter, low, across, preferred_element_type=jnp.float32)
    chosen = by_irrep[:blocks]
    for g in range(1, IRREPS):
        chosen = jnp.where(own_row == g, by_irrep[g * blocks : (g + 1) * blocks], chosen)
    return chosen


def tile(t_cols, right, column, ab_row, residual):
    high, low = pieces(t_cols.T)
    left = jnp.concatenate([high, low, high, low], axis=1)
    total = jnp.dot(left, right, preferred_element_type=jnp.float32)
    same = jnp.concatenate([column] * (ab_row.shape[1] // LANES), axis=1) == ab_row
    return residual + jnp.where(same, total, jnp.float32(0))


def ladder_kernel(
    n_pair, n_virt, parts, v_parts,
    t_hbm, v_hbm, r_hbm, pi_hbm, ai_hbm, cdt_hbm, cdv_hbm,
    out_ref, t_last, right_ref, column_last, ai_ref,
    t_own, v_own, pi_ref, cdt_ref, cdv_ref, t_all, v_all, column_ref,
    load_sem, t_send, t_recv, tf_send, v_send, v_recv, vf_send,
):
    p, v = lax.axis_index("pair"), lax.axis_index("virt")
    a, b = v // 2, v % 2
    c, k = p // 2, p % 2
    n_a, n_c = n_virt // 2, n_pair // 2
    rows, t_width = t_own.shape
    ab, v_width = v_own.shape
    t_blocks, v_blocks = t_width // IRREPS, v_width // IRREPS
    blocks = t_all.shape[0]

    barrier = pltpu.get_barrier_semaphore()

    def greet(dev):
        pl.semaphore_signal(barrier, inc=1, device_id=dev, device_id_type=MESH)

    far_a = [nth_other(n_a, a, s) for s in range(n_a - 1)]
    far_c = [nth_other(n_c, c, s) for s in range(n_c - 1)]
    for o in far_a:
        greet((p, o * 2 + b))
    greet((p, a * 2 + 1 - b))
    for o in far_c:
        greet((o * 2 + k, v))
    greet((c * 2 + 1 - k, v))

    t_span, v_span = rows // parts, ab // v_parts

    def load(src, dst, n):
        copy = pltpu.make_async_copy(src, dst, load_sem.at[n])
        copy.start()
        return copy

    labels = [load(cdt_hbm, cdt_ref, 0), load(pi_hbm, pi_ref, 1)]
    t_loads = [
        load(t_hbm.at[pl.ds(h * t_span, t_span), :], t_own.at[pl.ds(h * t_span, t_span), :], 5 + h)
        for h in range(parts)
    ]
    v_loads = [load(cdv_hbm, cdv_ref, 2), load(ai_hbm, ai_ref, 3), load(v_hbm, v_own, 4)]

    def copy(ref, owner, count, part, span, send, recv, dev):
        at = ref.at[pl.ds(pl.multiple_of(owner * count, count), count), pl.ds(part * span, span)]
        return pltpu.make_async_remote_copy(
            src_ref=at, dst_ref=at, send_sem=send, recv_sem=recv, device_id=dev, device_id_type=MESH
        )

    def t_copy(owner, part, send, dev):
        return copy(t_all, owner, t_blocks, part, t_span, send, t_recv.at[owner * parts + part], dev)

    def v_copy(owner, part, send, dev):
        return copy(v_all, owner, v_blocks, part, v_span, send, v_recv.at[owner * v_parts + part], dev)

    def send_t(h):
        mine = [t_copy(v, h, t_send.at[s, h], (p, far_a[s] * 2 + b)) for s in reversed(range(n_a - 1))]
        beside = t_copy(v, h, t_send.at[n_a - 1, h], (p, a * 2 + 1 - b))
        for one in [*mine, beside]:
            one.start()
        sent.append(beside)
        return mine

    def pass_t(h, steps):
        for s in steps:
            onward = t_copy(far_a[s] * 2 + b, h, tf_send.at[s, h], (p, a * 2 + 1 - b))
            onward.wait_recv()
            onward.start()
            sent.append(onward)

    def pass_v(h):
        for s in range(n_c - 1):
            onward = v_copy(far_c[s] * 2 + k, h, vf_send.at[s, h], (c * 2 + 1 - k, v))
            onward.wait_recv()
            onward.start()
            sent.append(onward)

    for one in labels:
        one.wait()
    cdt_row = irrep_row(cdt_ref, v * t_width // LANES, t_width) if t_width % LANES == 0 else cdt_ref[pl.ds(v, 1), :]
    sent = []
    for h in range(parts):
        t_loads[h].wait()
        own = irrep_row(pi_ref, h * t_span // LANES, t_span)
        t_all[pl.ds(pl.multiple_of(v * t_blocks, t_blocks), t_blocks), h * t_span : (h + 1) * t_span] = pick(
            cdt_row, t_own[h * t_span : (h + 1) * t_span, :], own
        )
        if h == 0:
            pl.semaphore_wait(barrier, n_a + n_c)
        sent.extend(send_t(h))

    for one in v_loads:
        one.wait()
    load_r = load(r_hbm, out_ref, 5 + parts)
    cdv_row = irrep_row(cdv_ref, p * v_width // LANES, v_width) if v_width % LANES == 0 else cdv_ref[pl.ds(p, 1), :]
    for h in range(v_parts):
        own = irrep_row(ai_ref, h * v_span // LANES, v_span)
        v_all[pl.ds(pl.multiple_of(p * v_blocks, v_blocks), v_blocks), h * v_span : (h + 1) * v_span] = pick(
            cdv_row, v_own[h * v_span : (h + 1) * v_span, :], own
        )
        for s in reversed(range(n_c - 1)):
            sent.append(v_copy(p, h, v_send.at[s, h], (far_c[s] * 2 + k, v)))
            sent[-1].start()
        sent.append(v_copy(p, h, v_send.at[n_c - 1, h], (c * 2 + 1 - k, v)))
        sent[-1].start()

    for h in range(parts):
        pass_t(h, range(n_a - 1))
        pass_v(h)

    early = rows - t_last.shape[1]
    for m in range(rows // LANES):
        labels = jnp.broadcast_to(pi_ref[m : m + 1, :], (LANES, LANES)).T
        if m * LANES < early:
            column_ref[m * LANES : (m + 1) * LANES, :] = labels
        else:
            column_last[m * LANES - early : (m + 1) * LANES - early, :] = labels

    for h in range(v_parts):
        span = slice(h * v_span, (h + 1) * v_span)
        for o in range(n_c):
            v_copy(o * 2 + 1 - k, h, v_send.at[0, h], (p, v)).wait_recv()
        high, low = pieces(v_all[:, span])
        right_ref[:blocks, span] = high
        right_ref[blocks : 2 * blocks, span] = high
        right_ref[2 * blocks : 3 * blocks, span] = low
        right_ref[3 * blocks :, span] = low

    ab_row = irrep_row(ai_ref, 0, ab)
    load_r.wait()
    for h in range(parts):
        for o in range(n_a):
            t_copy(o * 2 + 1 - b, h, t_send.at[0, h], (p, v)).wait_recv()
        if h * t_span >= early:
            t_last[:, h * t_span - early : (h + 1) * t_span - early] = t_all[:, h * t_span : (h + 1) * t_span]
            continue
        for m in range(h * t_span // LANES, (h + 1) * t_span // LANES):
            at = slice(m * LANES, (m + 1) * LANES)
            out_ref[at, :] = tile(t_all[:, at], right_ref[...], column_ref[at, :], ab_row, out_ref[at, :])
    for s in sent:
        s.wait_send()


def ladder(n_pair, n_virt, t, v, residual, pi, ai, cd, cdt, cdv):
    parts, v_parts = 2, 2
    rows, t_width = t.shape
    ab, v_width = v.shape
    blocks = cd // IRREPS
    vmem, dma = pltpu.VMEM, pltpu.SemaphoreType.DMA
    n_a, n_c = n_virt // 2, n_pair // 2
    operands = (t, v, residual, pi, ai, cdt, cdv)
    return pl.pallas_call(
        functools.partial(ladder_kernel, n_pair, n_virt, parts, v_parts),
        out_shape=(
            vmem((rows, ab), jnp.float32),
            vmem((blocks, rows // 2), jnp.float32),
            vmem((4 * blocks, ab), jnp.bfloat16),
            vmem((rows // 2, LANES), jnp.int32),
            vmem(ai.shape, jnp.int32),
        ),
        in_specs=[pl.BlockSpec(memory_space=pltpu.HBM)] * len(operands),
        out_specs=(pl.BlockSpec(memory_space=vmem),) * 5,
        scratch_shapes=[
            vmem((rows, t_width), jnp.float32),
            vmem((ab, v_width), jnp.float32),
            vmem(pi.shape, jnp.int32),
            vmem(cdt.shape, jnp.int32),
            vmem(cdv.shape, jnp.int32),
            vmem((blocks, rows), jnp.float32),
            vmem((blocks, ab), jnp.float32),
            vmem((rows, LANES), jnp.int32),
            dma((6 + parts,)),
            dma((n_a, parts)),
            dma((n_virt * parts,)),
            dma((max(n_a - 1, 1), parts)),
            dma((n_c, v_parts)),
            dma((n_pair * v_parts,)),
            dma((max(n_c - 1, 1), v_parts)),
        ],
        compiler_params=pltpu.CompilerParams(
            collective_id=0, has_side_effects=True, vmem_limit_bytes=24 * 1024 * 1024
        ),
        name="pick_gather_ladder",
    )(*[pltpu.with_memory_space_constraint(x, pltpu.HBM) for x in operands])


def finish_kernel(parts, done, t_last, right_ref, column_last, ai_ref, dst, late, sem):
    rows, ab = done.shape
    late_rows = late.shape[0]
    early = rows - late_rows
    span = early // parts
    copies = [
        pltpu.make_async_copy(done.at[pl.ds(n * span, span), :], dst.at[pl.ds(n * span, span), :], sem.at[n])
        for n in range(parts)
    ]
    for c in copies:
        c.start()
    ab_row = irrep_row(ai_ref, 0, ab)
    for m in range(late_rows // LANES):
        at = slice(m * LANES, (m + 1) * LANES)
        row = early + m * LANES
        late[at, :] = tile(t_last[:, at], right_ref[...], column_last[at, :], ab_row, done[row : row + LANES, :])
        copies.append(
            pltpu.make_async_copy(late.at[pl.ds(m * LANES, LANES), :], dst.at[pl.ds(row, LANES), :], sem.at[parts + m])
        )
        copies[-1].start()
    for c in copies:
        c.wait()


def finish(done, t_last, *others):
    parts = 4
    late_rows = t_last.shape[1]
    operands = (done, t_last, *others)
    return pl.pallas_call(
        functools.partial(finish_kernel, parts),
        out_shape=jax.ShapeDtypeStruct(done.shape, done.dtype),
        in_specs=[pl.BlockSpec(memory_space=pltpu.VMEM)] * len(operands),
        out_specs=pl.BlockSpec(memory_space=pltpu.HBM),
        scratch_shapes=[
            pltpu.VMEM((late_rows, done.shape[1]), done.dtype),
            pltpu.SemaphoreType.DMA((parts + late_rows // LANES,)),
        ],
        compiler_params=pltpu.CompilerParams(vmem_limit_bytes=8 * 1024 * 1024),
        name="finish",
    )(*[pltpu.with_memory_space_constraint(x, pltpu.VMEM) for x in operands])


def solution(mesh):
    n_pair, n_virt = mesh.shape["pair"], mesh.shape["virt"]

    def shards(amplitudes, integrals, residual_in, pair_irrep, ab_irrep, cd_irrep):
        cd = cd_irrep.shape[0]
        pi, ai = pair_irrep.reshape(-1, LANES), ab_irrep.reshape(-1, LANES)

        def cd_rows(width):
            return cd_irrep.reshape(-1, LANES if width % LANES == 0 else width)

        return finish(
            *ladder(
                n_pair, n_virt, amplitudes, integrals, residual_in, pi, ai, cd,
                cd_rows(amplitudes.shape[1]), cd_rows(integrals.shape[1]),
            )
        )

    placed = (P("pair", "virt"), P("virt", "pair"), P("pair", "virt"), P("pair"), P("virt"), P())
    return jax.shard_map(
        shards, mesh=mesh, in_specs=placed, out_specs=P("pair", "virt"), check_vma=False
    )
```

```python
import functools

import jax
import jax.numpy as jnp
from jax import lax
from jax.experimental import pallas as pl
from jax.experimental.pallas import tpu as pltpu
from jax.sharding import PartitionSpec as P

IRREPS = 8
LANES = 128
MESH = pl.DeviceIdType.MESH


def pieces(x):
    high = x.astype(jnp.bfloat16)
    low = (x - high.astype(jnp.float32)).astype(jnp.bfloat16)
    return high, low


def nth_other(n, me, step):
    flip = me // (n // 2)
    mine = me + flip * (n - 1 - 2 * me)
    other = step + (step + n - mine) // n
    return other + flip * (n - 1 - 2 * other)


def irrep_row(rows_ref, first, count):
    n = count // LANES
    return jnp.concatenate([rows_ref[pl.ds(first + k, 1), :] for k in range(n)], axis=1)


def pick(cd_row, values, own_row):
    width = values.shape[1]
    blocks = width // IRREPS
    block = lax.broadcasted_iota(jnp.int32, (blocks, width), 0)
    lane_block = lax.shift_right_logical(lax.broadcasted_iota(jnp.int32, (blocks, width), 1), 3)
    slabs = [
        jnp.where((block == lane_block) & (cd_row == g), jnp.float32(1), jnp.float32(0))
        for g in range(IRREPS)
    ]
    sorter = jnp.concatenate(slabs, axis=0).astype(jnp.bfloat16)
    high, low = pieces(values)
    across = (((1,), (1,)), ((), ()))
    if width == LANES:
        both = jnp.concatenate([high, low], axis=1)
        twice = jnp.concatenate([sorter, sorter], axis=1)
        by_irrep = lax.dot_general(twice, both, across, preferred_element_type=jnp.float32)
    else:
        by_irrep = lax.dot_general(
            sorter, high, across, preferred_element_type=jnp.float32
        ) + lax.dot_general(sorter, low, across, preferred_element_type=jnp.float32)
    chosen = by_irrep[:blocks]
    for g in range(1, IRREPS):
        chosen = jnp.where(own_row == g, by_irrep[g * blocks : (g + 1) * blocks], chosen)
    return chosen


def tile(t_cols, right, column, ab_row, residual):
    high, low = pieces(t_cols.T)
    left = jnp.concatenate([high, low, high, low], axis=1)
    total = jnp.dot(left, right, preferred_element_type=jnp.float32)
    same = jnp.concatenate([column] * (ab_row.shape[1] // LANES), axis=1) == ab_row
    return residual + jnp.where(same, total, jnp.float32(0))


def ladder_kernel(
    n_pair, n_virt, parts, v_parts,
    t_hbm, v_hbm, r_hbm, pi_hbm, ai_hbm, cdt_hbm, cdv_hbm,
    out_ref, t_last, right_ref, column_last, ai_ref,
    t_own, v_own, pi_ref, cdt_ref, cdv_ref, t_all, v_all, column_ref,
    load_sem, t_send, t_recv, tf_send, v_send, v_recv, vf_send,
):
    p, v = lax.axis_index("pair"), lax.axis_index("virt")
    a, b = v // 2, v % 2
    c, k = p // 2, p % 2
    n_a, n_c = n_virt // 2, n_pair // 2
    rows, t_width = t_own.shape
    ab, v_width = v_own.shape
    t_blocks, v_blocks = t_width // IRREPS, v_width // IRREPS
    blocks = t_all.shape[0]

    barrier = pltpu.get_barrier_semaphore()

    def greet(dev):
        pl.semaphore_signal(barrier, inc=1, device_id=dev, device_id_type=MESH)

    far_a = [nth_other(n_a, a, s) for s in range(n_a - 1)]
    far_c = [nth_other(n_c, c, s) for s in range(n_c - 1)]
    for o in far_a:
        greet((p, o * 2 + b))
    greet((p, a * 2 + 1 - b))
    for o in far_c:
        greet((o * 2 + k, v))
    greet((c * 2 + 1 - k, v))

    t_span, v_span = rows // parts, ab // v_parts

    def load(src, dst, n):
        copy = pltpu.make_async_copy(src, dst, load_sem.at[n])
        copy.start()
        return copy

    labels = [load(cdt_hbm, cdt_ref, 0), load(pi_hbm, pi_ref, 1)]
    t_loads = [
        load(t_hbm.at[pl.ds(h * t_span, t_span), :], t_own.at[pl.ds(h * t_span, t_span), :], 5 + h)
        for h in range(parts)
    ]
    v_loads = [load(cdv_hbm, cdv_ref, 2), load(ai_hbm, ai_ref, 3), load(v_hbm, v_own, 4)]

    def copy(ref, owner, count, part, span, send, recv, dev):
        at = ref.at[pl.ds(pl.multiple_of(owner * count, count), count), pl.ds(part * span, span)]
        return pltpu.make_async_remote_copy(
            src_ref=at, dst_ref=at, send_sem=send, recv_sem=recv, device_id=dev, device_id_type=MESH
        )

    def t_copy(owner, part, send, dev):
        return copy(t_all, owner, t_blocks, part, t_span, send, t_recv.at[owner * parts + part], dev)

    def v_copy(owner, part, send, dev):
        return copy(v_all, owner, v_blocks, part, v_span, send, v_recv.at[owner * v_parts + part], dev)

    def send_t(h):
        mine = [t_copy(v, h, t_send.at[s, h], (p, far_a[s] * 2 + b)) for s in reversed(range(n_a - 1))]
        beside = t_copy(v, h, t_send.at[n_a - 1, h], (p, a * 2 + 1 - b))
        for one in [*mine, beside]:
            one.start()
        sent.append(beside)
        return mine

    def pass_t(h, steps):
        for s in steps:
            onward = t_copy(far_a[s] * 2 + b, h, tf_send.at[s, h], (p, a * 2 + 1 - b))
            onward.wait_recv()
            onward.start()
            sent.append(onward)

    def pass_v(h):
        for s in range(n_c - 1):
            onward = v_copy(far_c[s] * 2 + k, h, vf_send.at[s, h], (c * 2 + 1 - k, v))
            onward.wait_recv()
            onward.start()
            sent.append(onward)

    for one in labels:
        one.wait()
    cdt_row = irrep_row(cdt_ref, v * t_width // LANES, t_width) if t_width % LANES == 0 else cdt_ref[pl.ds(v, 1), :]
    sent = []
    def start_t(h):
        t_loads[h].wait()
        own = irrep_row(pi_ref, h * t_span // LANES, t_span)
        t_all[pl.ds(pl.multiple_of(v * t_blocks, t_blocks), t_blocks), h * t_span : (h + 1) * t_span] = pick(
            cdt_row, t_own[h * t_span : (h + 1) * t_span, :], own
        )
        if h == 0:
            pl.semaphore_wait(barrier, n_a + n_c)
        sent.extend(send_t(h))

    def start_v(h):
        own = irrep_row(ai_ref, h * v_span // LANES, v_span)
        v_all[pl.ds(pl.multiple_of(p * v_blocks, v_blocks), v_blocks), h * v_span : (h + 1) * v_span] = pick(
            cdv_row, v_own[h * v_span : (h + 1) * v_span, :], own
        )
        for s in reversed(range(n_c - 1)):
            sent.append(v_copy(p, h, v_send.at[s, h], (far_c[s] * 2 + k, v)))
            sent[-1].start()
        sent.append(v_copy(p, h, v_send.at[n_c - 1, h], (c * 2 + 1 - k, v)))
        sent[-1].start()

    start_t(0)
    for one in v_loads:
        one.wait()
    load_r = load(r_hbm, out_ref, 5 + parts)
    cdv_row = irrep_row(cdv_ref, p * v_width // LANES, v_width) if v_width % LANES == 0 else cdv_ref[pl.ds(p, 1), :]
    start_v(0)
    start_t(1)
    start_v(1)

    for h in range(parts):
        pass_t(h, range(n_a - 1))
        pass_v(h)

    early = rows - t_last.shape[1]
    for m in range(rows // LANES):
        labels = jnp.broadcast_to(pi_ref[m : m + 1, :], (LANES, LANES)).T
        if m * LANES < early:
            column_ref[m * LANES : (m + 1) * LANES, :] = labels
        else:
            column_last[m * LANES - early : (m + 1) * LANES - early, :] = labels

    for h in range(v_parts):
        span = slice(h * v_span, (h + 1) * v_span)
        for o in range(n_c):
            v_copy(o * 2 + 1 - k, h, v_send.at[0, h], (p, v)).wait_recv()
        high, low = pieces(v_all[:, span])
        right_ref[:blocks, span] = high
        right_ref[blocks : 2 * blocks, span] = high
        right_ref[2 * blocks : 3 * blocks, span] = low
        right_ref[3 * blocks :, span] = low

    ab_row = irrep_row(ai_ref, 0, ab)
    load_r.wait()
    for h in range(parts):
        for o in range(n_a):
            t_copy(o * 2 + 1 - b, h, t_send.at[0, h], (p, v)).wait_recv()
        if h == 0:
            at = slice(0, early)
            out_ref[at, :] = tile(t_all[:, at], right_ref[...], column_ref[...], ab_row, out_ref[at, :])
        first = max(h * t_span, early)
        t_last[:, first - early : (h + 1) * t_span - early] = t_all[:, first : (h + 1) * t_span]
    for s in sent:
        s.wait_send()


def ladder(n_pair, n_virt, t, v, residual, pi, ai, cd, cdt, cdv):
    parts, v_parts = 2, 2
    rows, t_width = t.shape
    ab, v_width = v.shape
    blocks = cd // IRREPS
    vmem, dma = pltpu.VMEM, pltpu.SemaphoreType.DMA
    n_a, n_c = n_virt // 2, n_pair // 2
    operands = (t, v, residual, pi, ai, cdt, cdv)
    return pl.pallas_call(
        functools.partial(ladder_kernel, n_pair, n_virt, parts, v_parts),
        out_shape=(
            vmem((rows, ab), jnp.float32),
            vmem((blocks, rows - rows // 4), jnp.float32),
            vmem((4 * blocks, ab), jnp.bfloat16),
            vmem((rows - rows // 4, LANES), jnp.int32),
            vmem(ai.shape, jnp.int32),
        ),
        in_specs=[pl.BlockSpec(memory_space=pltpu.HBM)] * len(operands),
        out_specs=(pl.BlockSpec(memory_space=vmem),) * 5,
        scratch_shapes=[
            vmem((rows, t_width), jnp.float32),
            vmem((ab, v_width), jnp.float32),
            vmem(pi.shape, jnp.int32),
            vmem(cdt.shape, jnp.int32),
            vmem(cdv.shape, jnp.int32),
            vmem((blocks, rows), jnp.float32),
            vmem((blocks, ab), jnp.float32),
            vmem((rows // 4, LANES), jnp.int32),
            dma((6 + parts,)),
            dma((n_a, parts)),
            dma((n_virt * parts,)),
            dma((max(n_a - 1, 1), parts)),
            dma((n_c, v_parts)),
            dma((n_pair * v_parts,)),
            dma((max(n_c - 1, 1), v_parts)),
        ],
        compiler_params=pltpu.CompilerParams(
            collective_id=0, has_side_effects=True, vmem_limit_bytes=24 * 1024 * 1024
        ),
        name="pick_gather_ladder",
    )(*[pltpu.with_memory_space_constraint(x, pltpu.HBM) for x in operands])


def finish_kernel(parts, tiles, done, t_last, right_ref, column_last, ai_ref, dst, late, sem):
    rows, ab = done.shape
    late_rows = late.shape[0]
    early = rows - late_rows
    span = early // parts
    copies = [
        pltpu.make_async_copy(done.at[pl.ds(n * span, span), :], dst.at[pl.ds(n * span, span), :], sem.at[n])
        for n in range(parts)
    ]
    for c in copies:
        c.start()
    ab_row = irrep_row(ai_ref, 0, ab)
    step = late.shape[0] // tiles
    for m in range(tiles):
        at = slice(m * step, (m + 1) * step)
        row = early + m * step
        late[at, :] = tile(t_last[:, at], right_ref[...], column_last[at, :], ab_row, done[row : row + step, :])
        copies.append(
            pltpu.make_async_copy(late.at[pl.ds(m * step, step), :], dst.at[pl.ds(row, step), :], sem.at[parts + m])
        )
        copies[-1].start()
    for c in copies:
        c.wait()


def finish(done, t_last, *others):
    parts, tiles = 2, 3
    late_rows = t_last.shape[1]
    operands = (done, t_last, *others)
    return pl.pallas_call(
        functools.partial(finish_kernel, parts, tiles),
        out_shape=jax.ShapeDtypeStruct(done.shape, done.dtype),
        in_specs=[pl.BlockSpec(memory_space=pltpu.VMEM)] * len(operands),
        out_specs=pl.BlockSpec(memory_space=pltpu.HBM),
        scratch_shapes=[
            pltpu.VMEM((late_rows, done.shape[1]), done.dtype),
            pltpu.SemaphoreType.DMA((parts + tiles,)),
        ],
        compiler_params=pltpu.CompilerParams(vmem_limit_bytes=12 * 1024 * 1024),
        name="finish",
    )(*[pltpu.with_memory_space_constraint(x, pltpu.VMEM) for x in operands])


def solution(mesh):
    n_pair, n_virt = mesh.shape["pair"], mesh.shape["virt"]

    def shards(amplitudes, integrals, residual_in, pair_irrep, ab_irrep, cd_irrep):
        cd = cd_irrep.shape[0]
        pi, ai = pair_irrep.reshape(-1, LANES), ab_irrep.reshape(-1, LANES)

        def cd_rows(width):
            return cd_irrep.reshape(-1, LANES if width % LANES == 0 else width)

        return finish(
            *ladder(
                n_pair, n_virt, amplitudes, integrals, residual_in, pi, ai, cd,
                cd_rows(amplitudes.shape[1]), cd_rows(integrals.shape[1]),
            )
        )

    placed = (P("pair", "virt"), P("virt", "pair"), P("pair", "virt"), P("pair"), P("virt"), P())
    return jax.shard_map(
        shards, mesh=mesh, in_specs=placed, out_specs=P("pair", "virt"), check_vma=False
    )
```
